128 devices in a mesh: dp: 16 (over y, z), tensor: 8 (over x, core).
Axes of the slice: x: 4, y: 4, z: 4, core: 2. Of those that a mesh axis runs over, the one named last changes fastest.
Arguments:
- residual: bfloat16 [2048, 8192], P('dp', 'tensor'), may hold values from -6 to 6
- partials: bfloat16 [8, 2048, 8192], P('tensor', 'dp'), may hold values from -4 to 4
- low_features: bfloat16 [2048, 8192], P('dp', 'tensor'), may hold values from -6 to 6
- mid_features: bfloat16 [2048, 8192], P('dp', 'tensor'), may hold values from -6 to 6
- join_weight: bfloat16 [3, 8192, 8192], P(None, 'tensor', 'dp'), may hold values from -0.0390625 to 0.0390625
- lengths: int32 [16, 5], replicated, may hold values from 16 to 32, as said below
- shard_of: int32 [16, 5], replicated, may hold values from 0 to 15, as said below
- joined_cotangent: bfloat16 [2048, 8192], P('tensor', 'dp'), may hold values from -0.19921875 to 0.19921875
Outputs:
- routed_rows: bfloat16 [16, 16, 32, 8192], P('dp', 'tensor')
- join_grad: float32 [3, 8192, 8192], P(None, 'tensor', 'dp')
The draws below stay inside these ranges and needn't reach their ends.
Inputs may be any that keep to these rules, and one draw needn't show every extreme that they name: Row p holds the lengths of pack p's 5 conversations in token order; each row sums to 128 and its largest entry is exactly 32. `shard_of`: the conversations of one pack go to distinct draft shards, and every pack sends one of its conversations of length 32 to one common shard (a pack may hold more than one conversation of length 32; only one of them goes to the common shard).
All inputs are finite; a program needn't handle non-finite values.
Results may differ from the reference program's by a relative error of at most 0.015.
Values may be sent and summed in bfloat16 or wider, within the bound.
A program may use at most 128 MiB of HBM per device.

```python
import jax
import jax.numpy as jnp

D = 8192
CONV = 5
TOK_DEV = 128
MAXLEN = 32
TOKENS = 2048
N_DP = 16
N_TENSOR = 8


def pack_plan(key):
    key_spread = jax.random.fold_in(key, 11)
    key_place = jax.random.fold_in(key, 12)
    key_common = jax.random.fold_in(key, 13)
    key_order = jax.random.fold_in(key, 14)
    quarter = MAXLEN // 4
    middle = 3 * quarter
    spread = jax.random.randint(key_spread, (N_DP, 2), 0, quarter + 1).astype(jnp.int32)
    four = jnp.stack([middle - spread[:, 0], middle + spread[:, 0], middle - spread[:, 1], middle + spread[:, 1]], axis=1)
    place = jax.random.randint(key_place, (N_DP, 1), 0, CONV).astype(jnp.int32)
    positions = jnp.arange(CONV, dtype=jnp.int32)[None, :]
    others_at = jnp.clip(positions - (positions > place).astype(jnp.int32), 0, 3)
    lengths = jnp.where(positions == place, MAXLEN, jnp.take_along_axis(four, others_at, axis=1)).astype(jnp.int32)
    common = jax.random.randint(key_common, (), 0, N_DP).astype(jnp.int32)
    scores = jax.random.randint(key_order, (N_DP, N_DP - 1), 0, 1 << 20).astype(jnp.int32) * (N_DP - 1)
    scores = scores + jnp.arange(N_DP - 1, dtype=jnp.int32)[None, :]
    ordered = jnp.argsort(scores, axis=1, stable=True)[:, :CONV - 1].astype(jnp.int32)
    shards = ordered + (ordered >= common).astype(jnp.int32)
    shard_of = jnp.where(positions == place, common, jnp.take_along_axis(shards, others_at, axis=1)).astype(jnp.int32)
    return (lengths, shard_of)


def draw_lengths(key, part):
    return pack_plan(key)[0]


def draw_shard_of(key, part):
    return pack_plan(key)[1]


def levels(own_key, extent, cuts, least, largest):
    gain, own = 1.0, jax.random.fold_in(own_key, 6)
    for axis_at, blocks in cuts:
        heights = jnp.exp(jax.random.uniform(jax.random.fold_in(own, axis_at), (blocks,), jnp.float32, least / len(cuts), largest / len(cuts)))
        gain = gain * jnp.repeat(heights, extent[axis_at] // blocks).reshape([-1 if axis == axis_at else 1 for axis in range(len(extent))])
    return gain


def gaussian(key, dims, deviation, reach, split=(), kind=jnp.bfloat16):
    entries = jax.random.normal(key, dims, jnp.float32) * deviation
    if len(split) > 0:
        entries = levels(key, dims, split, -0.22, 0.18) * entries
    return jnp.clip(entries, min=-reach, max=reach).astype(kind)


def setup_inputs(seed: int = 0) -> dict:
    streams_of = jax.random.split(jax.random.key(seed), 9)
    residual = gaussian(streams_of[0], (TOKENS, D), 1.0, 6.0, ((0, 16), (1, 8)))
    partials = gaussian(streams_of[1], (N_TENSOR, TOKENS, D), 0.5, 4.0, ((0, 8), (1, 16)))
    low_features = gaussian(streams_of[2], (TOKENS, D), 1.0, 6.0, ((0, 16), (1, 8)))
    mid_features = gaussian(streams_of[3], (TOKENS, D), 1.0, 6.0, ((0, 16), (1, 8)))
    join_weight = gaussian(streams_of[4], (3, D, D), (3 * D) ** -0.5, 0.0390625, ((1, 8), (2, 16)))
    lengths = draw_lengths(jax.random.fold_in(streams_of[8], 71), 0)
    shard_of = draw_shard_of(jax.random.fold_in(streams_of[8], 71), 0)
    joined_cotangent = gaussian(streams_of[7], (TOKENS, D), 0.03, 0.19921875, ((0, 8), (1, 16)))
    return dict(residual=residual, partials=partials, low_features=low_features, mid_features=mid_features, join_weight=join_weight, lengths=lengths, shard_of=shard_of, joined_cotangent=joined_cotangent)


def build_slots(block, lengths, shard_of, shard_count, longest, pack_tokens):
    starts = jnp.cumsum(lengths, axis=1) - lengths
    shards = jnp.arange(shard_count, dtype=jnp.int32)
    match = (shard_of[None, :, :] == shards[:, None, None]).astype(jnp.int32)
    first = jnp.sum(match * starts[None, :, :], axis=2)
    count = jnp.sum(match * lengths[None, :, :], axis=2)
    offsets = jnp.arange(longest, dtype=jnp.int32)
    packs = jnp.arange(lengths.shape[0], dtype=jnp.int32)
    source = packs[None, :, None] * pack_tokens + first[:, :, None] + offsets[None, None, :]
    valid = offsets[None, None, :] < count[:, :, None]
    source = jnp.clip(source, 0, block.shape[0] - 1).astype(jnp.int32)
    picked = jnp.take(block, source.reshape(-1), axis=0)
    picked = picked.reshape(source.shape + (block.shape[1],))
    return jnp.where(valid[..., None], picked, jnp.zeros((), block.dtype))


def reference(residual, partials, low_features, mid_features, join_weight, lengths, shard_of, joined_cotangent):
    summed = residual.astype(jnp.float32) + jnp.sum(partials.astype(jnp.float32), axis=0)
    top_features = summed.astype(jnp.bfloat16)
    stacked = jnp.stack([low_features, mid_features, top_features], axis=1).reshape(TOKENS, 3 * D)
    joined = jnp.dot(stacked, join_weight.reshape(3 * D, D), preferred_element_type=jnp.float32).astype(jnp.bfloat16)
    routed_rows = build_slots(joined, lengths, shard_of, N_DP, MAXLEN, TOK_DEV)
    join_grad = jnp.dot(stacked.T, joined_cotangent, preferred_element_type=jnp.float32).reshape(3, D, D)
    return routed_rows, join_grad
```

```python
import jax
import jax.numpy as jnp
from jax import lax
from jax.experimental import pallas as pl
from jax.experimental.pallas import tpu as pltpu
from jax.sharding import PartitionSpec as P

MESH = pl.DeviceIdType.MESH

KIND = (0, 1, 0, 1, 2, 0, 2, 1, 2, 0, 1, 2)
WAVE = (0, 0, 1, 1, 0, 2, 1, 2, 2, 3, 3, 3)
SLOTS = len(KIND)
FIRST_TOP = 4
NEXT = tuple(
    next((b2 for b2 in range(SLOTS) if KIND[b2] == KIND[b] and WAVE[b2] == WAVE[b] + 1), 0)
    for b in range(SLOTS)
)
CHUNKS = 4
GRAD_LAG = 6


def lut(values, index):
    out = jnp.int32(values[0])
    for i in range(1, len(values)):
        step = values[i] - values[i - 1]
        if step:
            out = out + jnp.where(index >= i, jnp.int32(step), jnp.int32(0))
    return out


def div(a, b):
    return lax.div(a, jnp.int32(b))


def rem(a, b):
    return lax.rem(a, jnp.int32(b))


def ring_position(ring, y, z):
    turn = rem(y + z, 4)
    return 4 * (y + div(ring, 2) * (z - y)) + turn


def ring_device(ring, position):
    u = div(position, 4)
    v = rem(rem(position, 4) - u + 8, 4)
    half = div(ring, 2)
    return 4 * (u + half * (v - u)) + (v + half * (u - v))


def kernel(
    residual, partials, low, mid, weight, cot, lengths, shards,
    routed, grad,
    blocks, w_buf, cot_buf, mate_buf, own_buf, sum_buf, x_buf, res_buf,
    joined, part_buf, owner_buf, slot_buf, select_buf, grad_buf,
    load_sem, mate_send, mate_recv, x_send, x_recv, ring_send, ring_recv,
    cot_send, cot_recv, part_send, part_recv, route_send, route_recv, grad_sem,
):
    d = lax.axis_index("dp")
    s = lax.axis_index("tensor")
    y, z = div(d, 4), rem(d, 4)
    x, core = div(s, 2), rem(s, 2)
    cls = rem(y + z, 4)

    ring_of = [
        rem(cls + a % 2, 2) + 2 * rem(div(cls, 2) + a // 2, 2) for a in range(4)
    ]
    sign_of = [1 - 2 * rem(ring, 2) for ring in ring_of]
    place_of = [ring_position(ring, y, z) for ring in ring_of]
    target_of = [
        ring_device(ring_of[a], rem(place_of[a] + sign_of[a] + 16, 16)) for a in range(4)
    ]

    def pack_of(a, wave):
        place = rem(place_of[a] - sign_of[a] * (4 * wave + a) + 32, 16)
        return ring_device(ring_of[a], place)

    def slot_of(pack):
        py, pz = div(pack, 4), rem(pack, 4)
        ring = rem(py + pz, 4)
        sign = 1 - 2 * rem(ring, 2)
        gap = rem(sign * (ring_position(ring, y, z) - ring_position(ring, py, pz)) + 32, 16)
        return div(gap, 4), rem(gap, 4)

    load_low = pltpu.make_async_copy(low, blocks.at[0, 0], load_sem.at[0])
    load_mid = pltpu.make_async_copy(mid, blocks.at[1, 0], load_sem.at[1])
    load_res = pltpu.make_async_copy(residual, res_buf, load_sem.at[2])
    load_w = pltpu.make_async_copy(weight, w_buf, load_sem.at[3])

    def columns(delta, which):
        chip = rem(x + delta, 4)
        start = pl.multiple_of((2 * chip + which) * 1024, 1024)
        return partials.at[0, :, pl.ds(start, 1024)]

    load_own = [
        pltpu.make_async_copy(columns(delta, core), own_buf.at[delta], load_sem.at[4 + delta])
        for delta in range(4)
    ]
    load_low.start()
    for delta in (2, 1, 3, 0):
        load_own[delta].start()
    load_mid.start()
    load_res.start()
    load_w.start()

    barrier = pltpu.get_barrier_semaphore()

    @pl.loop(1, 16)
    def _(step):
        pl.semaphore_signal(
            barrier, inc=1, device_id=(rem(d + step, 16), s), device_id_type=MESH
        )

    @pl.loop(1, 8)
    def _(step):
        pl.semaphore_signal(
            barrier, inc=1, device_id=(d, rem(s + step, 8)), device_id_type=MESH
        )

    for j in range(2):
        pack = 2 * s + j
        row = lax.broadcasted_iota(jnp.int32, (512, 128), 0)
        token = lax.broadcasted_iota(jnp.int32, (512, 128), 1)
        shard = jnp.right_shift(row, 5)
        offset = jnp.bitwise_and(row, 31)
        source = jnp.full((512, 128), -1, jnp.int32)
        start = jnp.int32(0)
        for conv in range(5):
            count = lengths[pack, conv]
            here = (shard == shards[pack, conv]) & (offset < count)
            source = jnp.where(here, start + offset, source)
            start = start + count
        select_buf[j] = jnp.where(source == token, 1.0, 0.0).astype(jnp.bfloat16)

    pl.semaphore_wait(barrier, 22)

    mate = (d, s + 1 - 2 * core)
    mate_copies = [
        pltpu.make_async_remote_copy(
            src_ref=columns(delta, 1 - core),
            dst_ref=mate_buf.at[delta],
            send_sem=mate_send.at[delta],
            recv_sem=mate_recv.at[delta],
            device_id=mate,
            device_id_type=MESH,
        )
        for delta in range(4)
    ]
    for delta in (2, 1, 3, 0):
        mate_copies[delta].start()

    def forward(a, b, chunk):
        rows = pl.ds(32 * chunk, 32)
        to_b, to_a = (b, a + 1) if a < 3 else (lut(NEXT, b), 0)
        pltpu.make_async_remote_copy(
            src_ref=blocks.at[b, a, rows],
            dst_ref=blocks.at[to_b, to_a, rows],
            send_sem=ring_send.at[a],
            recv_sem=ring_recv.at[to_b, to_a, chunk],
            device_id=(target_of[a], s),
            device_id_type=MESH,
        ).start()

    load_low.wait()
    for chunk in range(CHUNKS):
        forward(0, jnp.int32(0), chunk)
    load_mid.wait()
    for chunk in range(CHUNKS):
        forward(0, jnp.int32(1), chunk)

    x_copies = {}
    for delta in (2, 1, 3, 0):
        load_own[delta].wait()
        mate_copies[delta].wait_recv()
        sum_buf[delta] = (
            own_buf[delta].astype(jnp.float32) + mate_buf[delta].astype(jnp.float32)
        ).astype(jnp.bfloat16)
        if delta:
            x_copies[delta] = pltpu.make_async_remote_copy(
                src_ref=sum_buf.at[delta],
                dst_ref=x_buf.at[delta - 1],
                send_sem=x_send.at[delta - 1],
                recv_sem=x_recv.at[delta - 1],
                device_id=(d, 2 * rem(x + delta, 4) + core),
                device_id_type=MESH,
            )
            x_copies[delta].start()

    load_w.wait()
    load_res.wait()

    def own_top():
        for delta in (1, 2, 3):
            x_copies[delta].wait_recv()
        total = res_buf[...].astype(jnp.float32) + sum_buf[0].astype(jnp.float32)
        for delta in (1, 2, 3):
            total = total + x_buf[delta - 1].astype(jnp.float32)
        blocks[FIRST_TOP, 0] = total.astype(jnp.bfloat16)
        for chunk in range(CHUNKS):
            forward(0, jnp.int32(FIRST_TOP), chunk)
        for j in range(2):
            wave, stream = slot_of(2 * s + j)
            rows = cot.at[pl.ds(128 * j, 128)]
            pltpu.make_async_copy(rows, cot_buf.at[wave, stream], cot_recv).start()

            @pl.loop(1, 8)
            def _(step):
                pltpu.make_async_remote_copy(
                    src_ref=rows,
                    dst_ref=cot_buf.at[wave, stream],
                    send_sem=cot_send,
                    recv_sem=cot_recv,
                    device_id=(d, rem(s + step, 8)),
                    device_id_type=MESH,
                ).start()

    def handle(a, b, chunk):
        valid = (b >= 0) & (b < SLOTS)
        if a == 0:
            valid = valid & (b >= 2) & (b != FIRST_TOP)

        @pl.when(valid)
        def _():
            here = blocks.at[b, a, pl.ds(32 * chunk, 32)]
            pltpu.make_async_copy(here, here, ring_recv.at[b, a, chunk]).wait()
            if a < 3:
                forward(a, b, chunk)
            else:

                @pl.when(b < 9)
                def _():
                    forward(a, b, chunk)

    def joined_piece(b, kind, wave, piece):
        half, side = piece // 2, piece % 2
        rows = blocks[b, pl.ds(2 * half, 2)].reshape(256, 1024)
        product = jnp.dot(
            rows, w_buf[kind, :, pl.ds(256 * side, 256)], preferred_element_type=jnp.float32
        )
        at = (wave, pl.ds(256 * half, 256), pl.ds(256 * side, 256))
        joined[at] = jnp.where(kind == 0, 0.0, joined[at]) + product

    def grad_piece(b, piece):
        kind, wave = lut(KIND, b), lut(WAVE, b)
        rows = blocks[b, :, :, pl.ds(256 * piece, 256)].reshape(512, 256)
        product = lax.dot_general(
            rows,
            cot_buf[wave].reshape(512, 512),
            (((0,), (0,)), ((), ())),
            preferred_element_type=jnp.float32,
        )
        at = (kind, pl.ds(256 * piece, 256))
        grad_buf[at] = jnp.where(wave == 0, 0.0, grad_buf[at]) + product

    def send_parts(wave):
        for a in range(4):
            part_buf[wave, a] = joined[wave, pl.ds(128 * a, 128)].astype(jnp.bfloat16)
            pack = pack_of(a, wave)
            owner = div(pack, 2)
            there = owner_buf.at[rem(pack, 2), s]

            @pl.when(owner == s)
            def _():
                pltpu.make_async_copy(
                    part_buf.at[wave, a], there, part_recv.at[rem(pack, 2)]
                ).start()

            @pl.when(owner != s)
            def _():
                pltpu.make_async_remote_copy(
                    src_ref=part_buf.at[wave, a],
                    dst_ref=there,
                    send_sem=part_send,
                    recv_sem=part_recv.at[rem(pack, 2)],
                    device_id=(d, owner),
                    device_id_type=MESH,
                ).start()

    own_waves = [slot_of(2 * s + j)[0] for j in range(2)]

    def route(wave):
        for j in range(2):

            @pl.when(own_waves[j] == wave)
            def _():
                pltpu.make_async_copy(owner_buf.at[j], owner_buf.at[j], part_recv.at[j]).wait()
                total = owner_buf[j, 0].astype(jnp.float32)
                for t in range(1, 8):
                    total = total + owner_buf[j, t].astype(jnp.float32)
                slots = jnp.dot(
                    select_buf[j], total.astype(jnp.bfloat16), preferred_element_type=jnp.float32
                )
                slot_buf[j] = slots.astype(jnp.bfloat16).reshape(16, 32, 512)
                there = routed.at[0, j, :, pl.ds(pl.multiple_of(d * 512, 512), 512)]
                pltpu.make_async_copy(slot_buf.at[j, d], there, route_recv).start()

                @pl.loop(1, 16)
                def _(step):
                    shard = rem(d + step, 16)
                    pltpu.make_async_remote_copy(
                        src_ref=slot_buf.at[j, shard],
                        dst_ref=there,
                        send_sem=route_send,
                        recv_sem=route_recv,
                        device_id=(shard, s),
                        device_id_type=MESH,
                    ).start()

    def body(beta, carry):
        done = beta - 2
        kind, wave = lut(KIND, done), lut(WAVE, done)

        @pl.when(beta == FIRST_TOP)
        def _():
            own_top()

        @pl.when(beta == GRAD_LAG)
        def _():
            pltpu.make_async_copy(cot_buf, cot_buf, cot_recv).wait()

        for chunk in range(CHUNKS):
            for a in range(4):
                shift = chunk - 2 * a
                handle(a, beta + shift // CHUNKS, shift % CHUNKS)

            @pl.when(done >= 0)
            def _():
                joined_piece(done, kind, wave, chunk)

            @pl.when(beta >= GRAD_LAG)
            def _():
                grad_piece(beta - GRAD_LAG, chunk)

            if chunk == 0:
                @pl.when((beta == 7) | (beta == 9) | (beta == 11))
                def _():
                    route(div(beta - 7, 2))

        @pl.when((done >= 0) & (kind == 2))
        def _():
            send_parts(wave)

        return carry

    lax.fori_loop(0, SLOTS + 2, body, 0)

    def last(b, carry):
        for piece in range(4):
            grad_piece(b, piece)

        @pl.when(b >= 9)
        def _():
            kind = b - 9
            pltpu.make_async_copy(grad_buf.at[kind], grad.at[kind], grad_sem).start()

        return carry

    lax.fori_loop(SLOTS + 2 - GRAD_LAG, SLOTS, last, 0)
    route(jnp.int32(3))

    for delta in range(4):
        mate_copies[delta].wait_send()
    for delta in (1, 2, 3):
        x_copies[delta].wait_send()
    for a in range(4):
        sent = blocks.at[:, a] if a < 3 else blocks.at[pl.ds(0, 9), a]
        pltpu.make_async_copy(sent, sent, ring_send.at[a]).wait()
    sent = blocks.at[pl.ds(0, 7), 0]
    pltpu.make_async_copy(sent, sent, cot_send).wait()
    pltpu.make_async_copy(sent, sent, part_send).wait()
    pltpu.make_async_copy(grad_buf, grad_buf, grad_sem).wait()
    sent = slot_buf.at[:, pl.ds(0, 15)]
    pltpu.make_async_copy(sent, sent, route_send).wait()
    pltpu.make_async_copy(slot_buf, slot_buf, route_recv).wait()


def local(
    residual, partials, low_features, mid_features, join_weight, lengths, shard_of, joined_cotangent
):
    bf16, f32 = jnp.bfloat16, jnp.float32
    hbm = pl.BlockSpec(memory_space=pl.ANY)
    smem = pl.BlockSpec(memory_space=pltpu.SMEM)
    dma = pltpu.SemaphoreType.DMA
    return pl.pallas_call(
        kernel,
        out_shape=(
            jax.ShapeDtypeStruct((1, 2, 32, 8192), bf16),
            jax.ShapeDtypeStruct((3, 1024, 512), f32),
        ),
        in_specs=[hbm] * 6 + [smem] * 2,
        out_specs=(hbm, hbm),
        scratch_shapes=[
            pltpu.VMEM((SLOTS, 4, 128, 1024), bf16),
            pltpu.VMEM((3, 1024, 512), bf16),
            pltpu.VMEM((4, 4, 128, 512), bf16),
            pltpu.VMEM((4, 128, 1024), bf16),
            pltpu.VMEM((4, 128, 1024), bf16),
            pltpu.VMEM((4, 128, 1024), bf16),
            pltpu.VMEM((3, 128, 1024), bf16),
            pltpu.VMEM((128, 1024), bf16),
            pltpu.VMEM((4, 512, 512), f32),
            pltpu.VMEM((4, 4, 128, 512), bf16),
            pltpu.VMEM((2, 8, 128, 512), bf16),
            pltpu.VMEM((2, 16, 32, 512), bf16),
            pltpu.VMEM((2, 512, 128), bf16),
            pltpu.VMEM((3, 1024, 512), f32),
            dma((8,)),
            dma((4,)), dma((4,)),
            dma((3,)), dma((3,)),
            dma((4,)), dma((SLOTS, 4, CHUNKS)),
            dma, dma,
            dma, dma((2,)),
            dma, dma,
            dma,
        ],
        compiler_params=pltpu.CompilerParams(
            collective_id=0, has_side_effects=True, vmem_limit_bytes=56 * 1024 * 1024
        ),
    )(residual, partials, low_features, mid_features, join_weight, joined_cotangent, lengths, shard_of)


def solution(mesh):
    placed = (
        P("dp", "tensor"),
        P("tensor", "dp", None),
        P("dp", "tensor"),
        P("dp", "tensor"),
        P(None, "tensor", "dp"),
        P(),
        P(),
        P("tensor", "dp"),
    )
    return jax.shard_map(
        local,
        mesh=mesh,
        in_specs=placed,
        out_specs=(P("dp", "tensor", None, None), P(None, "tensor", "dp")),
        check_vma=False,
    )
```

```python
import jax
import jax.numpy as jnp
from jax import lax
from jax.experimental import pallas as pl
from jax.experimental.pallas import tpu as pltpu
from jax.sharding import PartitionSpec as P

MESH = pl.DeviceIdType.MESH

FAR_SLOT = (0, 1, 3, 2)
LOW, MID, TOP = 0, 1, 2


def lut(values, index):
    out = jnp.int32(values[0])
    for i in range(1, len(values)):
        step = values[i] - values[i - 1]
        if step:
            out = out + jnp.where(index >= i, jnp.int32(step), jnp.int32(0))
    return out


def div(a, b):
    return lax.div(a, jnp.int32(b))


def rem(a, b):
    return lax.rem(a, jnp.int32(b))


def kernel(
    residual, partials, low, mid, weight, cot, lengths, shards,
    routed, grad,
    blocks, w_buf, cot_buf, mate_buf, own_buf, sum_buf, x_buf, res_buf,
    joined, part_buf, owner_buf, slot_buf, select_buf, grad_buf,
    load_sem, mate_send, mate_recv, x_send, x_recv, ring_send, ring_recv,
    cot_send, cot_recv, part_send, part_recv, route_send, route_recv, grad_sem,
):
    d = lax.axis_index("dp")
    s = lax.axis_index("tensor")
    y, z = div(d, 4), rem(d, 4)
    x, core = div(s, 2), rem(s, 2)

    def slot_of(pack):
        return (
            lut(FAR_SLOT, rem(div(pack, 4) - y + 4, 4)),
            lut(FAR_SLOT, rem(rem(pack, 4) - z + 4, 4)),
        )

    def pack_of(i, j):
        return 4 * rem(y + FAR_SLOT[i], 4) + rem(z + FAR_SLOT[j], 4)

    ahead = (4 * rem(y + 1, 4) + z, 4 * y + rem(z + 1, 4))
    behind = (4 * rem(y + 3, 4) + z, 4 * y + rem(z + 3, 4))

    class Move:
        def __init__(self, kind, axis, half, fixed, op):
            self.kind, self.axis, self.half, self.fixed, self.op = kind, axis, half, fixed, op

        def at(self, slot, first, count):
            rows = pl.ds(64 * self.half + first, count)
            if self.axis == 0:
                return blocks.at[self.kind, slot, self.fixed, rows]
            return blocks.at[self.kind, self.fixed, slot, rows]

        def send(self, src, dst, sem, device):
            pltpu.make_async_remote_copy(
                src_ref=src,
                dst_ref=dst,
                send_sem=ring_send.at[self.kind],
                recv_sem=ring_recv.at[self.kind, self.op, sem],
                device_id=(device, s),
                device_id_type=MESH,
            ).start()

        def wait(self, ref, sem):
            pltpu.make_async_copy(ref, ref, ring_recv.at[self.kind, self.op, sem]).wait()

        def start(self):
            self.send(self.at(0, 0, 64), self.at(2, 0, 64), 0, ahead[self.axis])
            self.send(self.at(0, 0, 64), self.at(1, 0, 64), 1, behind[self.axis])

        def relay_ahead(self):
            self.wait(self.at(2, 0, 64), 0)
            self.send(self.at(2, 0, 32), self.at(3, 0, 32), 2, ahead[self.axis])

        def relay_behind(self):
            self.wait(self.at(1, 0, 64), 1)
            self.send(self.at(1, 32, 32), self.at(3, 32, 32), 3, behind[self.axis])

        def finish(self):
            self.wait(self.at(3, 0, 32), 2)
            self.wait(self.at(3, 32, 32), 3)

    first_y = [Move(kind, 0, 0, 0, 0) for kind in range(3)]
    first_z = [Move(kind, 1, 1, 0, 1) for kind in range(3)]
    then_z = [[Move(kind, 1, 0, i, 2 + i) for i in range(4)] for kind in range(3)]
    then_y = [[Move(kind, 0, 1, j, 6 + j) for j in range(4)] for kind in range(3)]

    def begin(kind):
        first_y[kind].start()
        first_z[kind].start()
        then_z[kind][0].start()
        then_y[kind][0].start()

    def spread(kind):
        first_y[kind].relay_ahead()
        then_z[kind][2].start()
        first_z[kind].relay_ahead()
        then_y[kind][2].start()
        first_y[kind].relay_behind()
        then_z[kind][1].start()
        first_z[kind].relay_behind()
        then_y[kind][1].start()

    def far(kind):
        first_y[kind].finish()
        then_z[kind][3].start()
        first_z[kind].finish()
        then_y[kind][3].start()

    def relay(kind, slot):
        then_z[kind][slot].relay_ahead()
        then_y[kind][slot].relay_ahead()
        then_z[kind][slot].relay_behind()
        then_y[kind][slot].relay_behind()

    def finish(kind, slots):
        for slot in slots:
            then_z[kind][slot].finish()
            then_y[kind][slot].finish()

    load_low = pltpu.make_async_copy(low, blocks.at[LOW, 0, 0], load_sem.at[0])
    load_mid = pltpu.make_async_copy(mid, blocks.at[MID, 0, 0], load_sem.at[1])
    load_res = pltpu.make_async_copy(residual, res_buf, load_sem.at[2])
    load_w = pltpu.make_async_copy(weight, w_buf, load_sem.at[3])

    def columns(delta, which):
        chip = rem(x + delta, 4)
        start = pl.multiple_of((2 * chip + which) * 1024, 1024)
        return partials.at[0, :, pl.ds(start, 1024)]

    load_own = [
        pltpu.make_async_copy(columns(delta, core), own_buf.at[delta], load_sem.at[4 + delta])
        for delta in range(4)
    ]
    load_low.start()
    for delta in (2, 1, 3, 0):
        load_own[delta].start()
    load_mid.start()
    load_res.start()
    load_w.start()

    barrier = pltpu.get_barrier_semaphore()

    @pl.loop(1, 16)
    def _(step):
        pl.semaphore_signal(
            barrier, inc=1, device_id=(rem(d + step, 16), s), device_id_type=MESH
        )

    @pl.loop(1, 8)
    def _(step):
        pl.semaphore_signal(
            barrier, inc=1, device_id=(d, rem(s + step, 8)), device_id_type=MESH
        )

    for j in range(2):
        pack = 2 * s + j
        row = lax.broadcasted_iota(jnp.int32, (512, 128), 0)
        token = lax.broadcasted_iota(jnp.int32, (512, 128), 1)
        shard = jnp.right_shift(row, 5)
        offset = jnp.bitwise_and(row, 31)
        source = jnp.full((512, 128), -1, jnp.int32)
        start = jnp.int32(0)
        for conv in range(5):
            count = lengths[pack, conv]
            here = (shard == shards[pack, conv]) & (offset < count)
            source = jnp.where(here, start + offset, source)
            start = start + count
        select_buf[j] = jnp.where(source == token, 1.0, 0.0).astype(jnp.bfloat16)

    pl.semaphore_wait(barrier, 22)

    mate = (d, s + 1 - 2 * core)
    mate_copies = [
        pltpu.make_async_remote_copy(
            src_ref=columns(delta, 1 - core),
            dst_ref=mate_buf.at[delta],
            send_sem=mate_send.at[delta],
            recv_sem=mate_recv.at[delta],
            device_id=mate,
            device_id_type=MESH,
        )
        for delta in range(4)
    ]
    for delta in (2, 1, 3, 0):
        mate_copies[delta].start()

    load_low.wait()
    begin(LOW)
    load_mid.wait()
    begin(MID)

    x_copies = {}
    for delta in (2, 1, 3, 0):
        load_own[delta].wait()
        mate_copies[delta].wait_recv()
        sum_buf[delta] = (
            own_buf[delta].astype(jnp.float32) + mate_buf[delta].astype(jnp.float32)
        ).astype(jnp.bfloat16)
        if delta:
            x_copies[delta] = pltpu.make_async_remote_copy(
                src_ref=sum_buf.at[delta],
                dst_ref=x_buf.at[delta - 1],
                send_sem=x_send.at[delta - 1],
                recv_sem=x_recv.at[delta - 1],
                device_id=(d, 2 * rem(x + delta, 4) + core),
                device_id_type=MESH,
            )
            x_copies[delta].start()

    load_w.wait()
    load_res.wait()

    def own_top():
        for delta in (1, 2, 3):
            x_copies[delta].wait_recv()
        total = res_buf[...].astype(jnp.float32) + sum_buf[0].astype(jnp.float32)
        for delta in (1, 2, 3):
            total = total + x_buf[delta - 1].astype(jnp.float32)
        blocks[TOP, 0, 0] = total.astype(jnp.bfloat16)

    def send_cot():
        for j in range(2):
            slot_y, slot_z = slot_of(2 * s + j)
            rows = cot.at[pl.ds(128 * j, 128)]
            pltpu.make_async_copy(rows, cot_buf.at[slot_y, slot_z], cot_recv).start()

            @pl.loop(1, 8)
            def _(step):
                pltpu.make_async_remote_copy(
                    src_ref=rows,
                    dst_ref=cot_buf.at[slot_y, slot_z],
                    send_sem=cot_send,
                    recv_sem=cot_recv,
                    device_id=(d, rem(s + step, 8)),
                    device_id_type=MESH,
                ).start()

    def joined_all(kind):
        @pl.loop(0, 4)
        def _(i):
            rows = blocks[kind, i].reshape(512, 1024)
            for side in range(2):
                columns = pl.ds(256 * side, 256)
                product = jnp.dot(
                    rows, w_buf[kind, :, columns], preferred_element_type=jnp.float32
                ).reshape(4, 128, 256)
                at = (pl.ds(4 * i, 4), slice(None), columns)
                joined[at] = product if kind == LOW else joined[at] + product

    def grad_all(kind):
        @pl.loop(0, 4)
        def _(piece):
            features = pl.ds(pl.multiple_of(256 * piece, 256), 256)
            grad_buf[kind, features] = lax.dot_general(
                blocks[kind, :, :, :, features].reshape(2048, 256),
                cot_buf[...].reshape(2048, 512),
                (((0,), (0,)), ((), ())),
                preferred_element_type=jnp.float32,
            )

        pltpu.make_async_copy(grad_buf.at[kind], grad.at[kind], grad_sem.at[kind]).start()

    def send_part(i, j):
        pack = pack_of(i, j)
        owner = div(pack, 2)
        there = owner_buf.at[rem(pack, 2), s]

        @pl.when(owner == s)
        def _():
            pltpu.make_async_copy(part_buf.at[i, j], there, part_recv.at[rem(pack, 2)]).start()

        @pl.when(owner != s)
        def _():
            pltpu.make_async_remote_copy(
                src_ref=part_buf.at[i, j],
                dst_ref=there,
                send_sem=part_send,
                recv_sem=part_recv.at[rem(pack, 2)],
                device_id=(d, owner),
                device_id_type=MESH,
            ).start()

    def joined_top(i, j, ni, nj):
        count = ni * nj
        rows = blocks[TOP, i:i + ni, j:j + nj].reshape(128 * count, 1024)
        product = jnp.dot(rows, w_buf[TOP], preferred_element_type=jnp.float32)
        product = product.reshape(count, 128, 512)
        for n in range(count):
            at = (i + n // nj, j + n % nj)
            total = joined[4 * at[0] + at[1]] + product[n]
            part_buf[at] = total.astype(jnp.bfloat16)
            send_part(*at)

    own_far = []
    for j in range(2):
        slot_y, slot_z = slot_of(2 * s + j)
        own_far.append((slot_y == 3) | (slot_z == 3))

    def route(is_far):
        for j in range(2):

            @pl.when(own_far[j] if is_far else jnp.logical_not(own_far[j]))
            def _():
                pltpu.make_async_copy(owner_buf.at[j], owner_buf.at[j], part_recv.at[j]).wait()
                total = owner_buf[j, 0].astype(jnp.float32)
                for t in range(1, 8):
                    total = total + owner_buf[j, t].astype(jnp.float32)
                slots = jnp.dot(
                    select_buf[j], total.astype(jnp.bfloat16), preferred_element_type=jnp.float32
                )
                slot_buf[j] = slots.astype(jnp.bfloat16).reshape(16, 32, 512)
                there = routed.at[0, j, :, pl.ds(pl.multiple_of(d * 512, 512), 512)]
                pltpu.make_async_copy(slot_buf.at[j, d], there, route_recv).start()

                @pl.loop(1, 16)
                def _(step):
                    shard = rem(d + step, 16)
                    pltpu.make_async_remote_copy(
                        src_ref=slot_buf.at[j, shard],
                        dst_ref=there,
                        send_sem=route_send,
                        recv_sem=route_recv,
                        device_id=(shard, s),
                        device_id_type=MESH,
                    ).start()

    spread(LOW)
    spread(MID)
    far(LOW)
    relay(LOW, 0)
    far(MID)
    own_top()
    begin(TOP)
    send_cot()
    relay(MID, 0)
    relay(LOW, 2)
    relay(LOW, 1)
    relay(MID, 2)
    relay(MID, 1)
    relay(LOW, 3)
    relay(MID, 3)
    finish(LOW, range(4))
    spread(TOP)
    joined_all(LOW)
    far(TOP)
    finish(MID, range(4))
    joined_all(MID)
    relay(TOP, 0)
    pltpu.make_async_copy(cot_buf, cot_buf, cot_recv).wait()
    grad_all(LOW)
    relay(TOP, 2)
    relay(TOP, 1)
    for i in range(3):
        joined_top(i, 0, 1, 3)
    relay(TOP, 3)
    grad_all(MID)
    route(False)
    finish(TOP, range(3))
    joined_top(0, 3, 3, 1)
    finish(TOP, (3,))
    joined_top(3, 0, 1, 4)
    grad_all(TOP)
    route(True)

    for delta in range(4):
        mate_copies[delta].wait_send()
    for delta in (1, 2, 3):
        x_copies[delta].wait_send()
    for kind in range(3):
        sent = joined.at[pl.ds(0, 15)]
        pltpu.make_async_copy(sent, sent, ring_send.at[kind]).wait()
    sent = joined.at[pl.ds(0, 7)]
    pltpu.make_async_copy(sent, sent, cot_send).wait()
    pltpu.make_async_copy(sent, sent, part_send).wait()
    for kind in range(3):
        pltpu.make_async_copy(grad_buf.at[kind], grad.at[kind], grad_sem.at[kind]).wait()
    sent = slot_buf.at[:, pl.ds(0, 15)]
    pltpu.make_async_copy(sent, sent, route_send).wait()
    pltpu.make_async_copy(slot_buf, slot_buf, route_recv).wait()


def local(
    residual, partials, low_features, mid_features, join_weight, lengths, shard_of, joined_cotangent
):
    bf16, f32 = jnp.bfloat16, jnp.float32
    hbm = pl.BlockSpec(memory_space=pl.ANY)
    smem = pl.BlockSpec(memory_space=pltpu.SMEM)
    dma = pltpu.SemaphoreType.DMA
    return pl.pallas_call(
        kernel,
        out_shape=(
            jax.ShapeDtypeStruct((1, 2, 32, 8192), bf16),
            jax.ShapeDtypeStruct((3, 1024, 512), f32),
        ),
        in_specs=[hbm] * 6 + [smem] * 2,
        out_specs=(hbm, hbm),
        scratch_shapes=[
            pltpu.VMEM((3, 4, 4, 128, 1024), bf16),
            pltpu.VMEM((3, 1024, 512), bf16),
            pltpu.VMEM((4, 4, 128, 512), bf16),
            pltpu.VMEM((4, 128, 1024), bf16),
            pltpu.VMEM((4, 128, 1024), bf16),
            pltpu.VMEM((4, 128, 1024), bf16),
            pltpu.VMEM((3, 128, 1024), bf16),
            pltpu.VMEM((128, 1024), bf16),
            pltpu.VMEM((16, 128, 512), f32),
            pltpu.VMEM((4, 4, 128, 512), bf16),
            pltpu.VMEM((2, 8, 128, 512), bf16),
            pltpu.VMEM((2, 16, 32, 512), bf16),
            pltpu.VMEM((2, 512, 128), bf16),
            pltpu.VMEM((3, 1024, 512), f32),
            dma((8,)),
            dma((4,)), dma((4,)),
            dma((3,)), dma((3,)),
            dma((3,)), dma((3, 10, 4)),
            dma, dma,
            dma, dma((2,)),
            dma, dma,
            dma((3,)),
        ],
        compiler_params=pltpu.CompilerParams(
            collective_id=0, has_side_effects=True, vmem_limit_bytes=56 * 1024 * 1024
        ),
    )(residual, partials, low_features, mid_features, join_weight, joined_cotangent, lengths, shard_of)


def solution(mesh):
    placed = (
        P("dp", "tensor"),
        P("tensor", "dp", None),
        P("dp", "tensor"),
        P("dp", "tensor"),
        P(None, "tensor", "dp"),
        P(),
        P(),
        P("tensor", "dp"),
    )
    return jax.shard_map(
        local,
        mesh=mesh,
        in_specs=placed,
        out_specs=(P("dp", "tensor", None, None), P(None, "tensor", "dp")),
        check_vma=False,
    )
```

```python
import jax
import jax.numpy as jnp
from jax import lax
from jax.experimental import pallas as pl
from jax.experimental.pallas import tpu as pltpu
from jax.sharding import PartitionSpec as P

MESH = pl.DeviceIdType.MESH

FAR_SLOT = (0, 1, 3, 2)
LOW, MID, TOP = 0, 1, 2


def lut(values, index):
    out = jnp.int32(values[0])
    for i in range(1, len(values)):
        step = values[i] - values[i - 1]
        if step:
            out = out + jnp.where(index >= i, jnp.int32(step), jnp.int32(0))
    return out


def div(a, b):
    return lax.div(a, jnp.int32(b))


def rem(a, b):
    return lax.rem(a, jnp.int32(b))


def kernel(
    residual, partials, low, mid, weight, cot, lengths, shards,
    routed, grad,
    blocks, w_buf, cot_buf, mate_buf, own_buf, sum_buf, x_buf, res_buf,
    joined, part_buf, owner_buf, slot_buf, select_buf, grad_buf, plan_buf, mate_part,
    load_sem, mate_send, mate_recv, x_send, x_recv, ring_send, ring_recv,
    cot_send, cot_recv, part_send, part_recv, pair_send, pair_recv, route_send, route_recv, grad_sem,
):
    d = lax.axis_index("dp")
    s = lax.axis_index("tensor")
    y, z = div(d, 4), rem(d, 4)
    x, core = div(s, 2), rem(s, 2)

    def slot_of(pack):
        return (
            lut(FAR_SLOT, rem(div(pack, 4) - y + 4, 4)),
            lut(FAR_SLOT, rem(rem(pack, 4) - z + 4, 4)),
        )

    def pack_of(i, j):
        return 4 * rem(y + FAR_SLOT[i], 4) + rem(z + FAR_SLOT[j], 4)

    ahead = (4 * rem(y + 1, 4) + z, 4 * y + rem(z + 1, 4))
    behind = (4 * rem(y + 3, 4) + z, 4 * y + rem(z + 3, 4))

    class Move:
        def __init__(self, kind, axis, half, fixed, op):
            self.kind, self.axis, self.half, self.fixed, self.op = kind, axis, half, fixed, op

        def at(self, slot, first, count):
            rows = pl.ds(64 * self.half + first, count)
            if self.axis == 0:
                return blocks.at[self.kind, slot, self.fixed, rows]
            return blocks.at[self.kind, self.fixed, slot, rows]

        def send(self, src, dst, sem, device):
            pltpu.make_async_remote_copy(
                src_ref=src,
                dst_ref=dst,
                send_sem=ring_send.at[self.kind],
                recv_sem=ring_recv.at[self.kind, self.op, sem],
                device_id=(device, s),
                device_id_type=MESH,
            ).start()

        def wait(self, ref, sem):
            pltpu.make_async_copy(ref, ref, ring_recv.at[self.kind, self.op, sem]).wait()

        def start(self):
            self.send(self.at(0, 0, 64), self.at(2, 0, 64), 0, ahead[self.axis])
            self.send(self.at(0, 0, 64), self.at(1, 0, 64), 1, behind[self.axis])

        def relay_ahead(self):
            self.wait(self.at(2, 0, 64), 0)
            self.send(self.at(2, 0, 32), self.at(3, 0, 32), 2, ahead[self.axis])

        def relay_behind(self):
            self.wait(self.at(1, 0, 64), 1)
            self.send(self.at(1, 32, 32), self.at(3, 32, 32), 3, behind[self.axis])

        def finish(self):
            self.wait(self.at(3, 0, 32), 2)
            self.wait(self.at(3, 32, 32), 3)

    first_y = [Move(kind, 0, 0, 0, 0) for kind in range(3)]
    first_z = [Move(kind, 1, 1, 0, 1) for kind in range(3)]
    then_z = [[Move(kind, 1, 0, i, 2 + i) for i in range(4)] for kind in range(3)]
    then_y = [[Move(kind, 0, 1, j, 6 + j) for j in range(4)] for kind in range(3)]

    def begin(kind):
        first_y[kind].start()
        first_z[kind].start()
        then_z[kind][0].start()
        then_y[kind][0].start()

    def spread(kind):
        first_y[kind].relay_ahead()
        then_z[kind][2].start()
        first_z[kind].relay_ahead()
        then_y[kind][2].start()
        first_y[kind].relay_behind()
        then_z[kind][1].start()
        first_z[kind].relay_behind()
        then_y[kind][1].start()

    def far_z(kind):
        first_y[kind].finish()
        then_z[kind][3].start()

    def far_y(kind):
        first_z[kind].finish()
        then_y[kind][3].start()

    def relay(kind, slot):
        then_z[kind][slot].relay_ahead()
        then_y[kind][slot].relay_ahead()
        then_z[kind][slot].relay_behind()
        then_y[kind][slot].relay_behind()

    def finish(kind, slots):
        for slot in slots:
            then_z[kind][slot].finish()
            then_y[kind][slot].finish()

    load_low = pltpu.make_async_copy(low, blocks.at[LOW, 0, 0], load_sem.at[0])
    load_mid = pltpu.make_async_copy(mid, blocks.at[MID, 0, 0], load_sem.at[1])
    load_lengths = pltpu.make_async_copy(lengths, plan_buf.at[0], load_sem.at[8])
    load_shards = pltpu.make_async_copy(shards, plan_buf.at[1], load_sem.at[9])
    load_res = pltpu.make_async_copy(residual, res_buf, load_sem.at[2])
    load_w = pltpu.make_async_copy(weight, w_buf, load_sem.at[3])

    def columns(delta, which):
        chip = rem(x + delta, 4)
        start = pl.multiple_of((2 * chip + which) * 1024, 1024)
        return partials.at[0, :, pl.ds(start, 1024)]

    load_own = [
        pltpu.make_async_copy(columns(delta, core), own_buf.at[delta], load_sem.at[4 + delta])
        for delta in range(4)
    ]
    load_low.start()
    load_lengths.start()
    load_shards.start()
    for delta in (2, 1, 3, 0):
        load_own[delta].start()
    load_mid.start()
    load_res.start()
    load_w.start()

    barrier = pltpu.get_barrier_semaphore()

    @pl.loop(1, 16)
    def _(step):
        pl.semaphore_signal(
            barrier, inc=1, device_id=(rem(d + step, 16), s), device_id_type=MESH
        )

    @pl.loop(1, 8)
    def _(step):
        pl.semaphore_signal(
            barrier, inc=1, device_id=(d, rem(s + step, 8)), device_id_type=MESH
        )

    load_lengths.wait()
    load_shards.wait()

    for j in range(2):
        pack = 2 * s + j
        row = lax.broadcasted_iota(jnp.int32, (512, 128), 0)
        token = lax.broadcasted_iota(jnp.int32, (512, 128), 1)
        shard = jnp.right_shift(row, 5)
        offset = jnp.bitwise_and(row, 31)
        source = jnp.full((512, 128), -1, jnp.int32)
        start = jnp.zeros((1, 1), jnp.int32)
        counts = plan_buf[0, pl.ds(pack, 1)]
        places = plan_buf[1, pl.ds(pack, 1)]
        for conv in range(5):
            count = counts[:, conv:conv + 1]
            here = (shard == places[:, conv:conv + 1]) & (offset < count)
            source = jnp.where(here, start + offset, source)
            start = start + count
        select_buf[j] = jnp.where(source == token, 1.0, 0.0).astype(jnp.bfloat16)

    pl.semaphore_wait(barrier, 22)

    mate = (d, s + 1 - 2 * core)
    mate_copies = [
        pltpu.make_async_remote_copy(
            src_ref=columns(delta, 1 - core),
            dst_ref=mate_buf.at[delta],
            send_sem=mate_send.at[delta],
            recv_sem=mate_recv.at[delta],
            device_id=mate,
            device_id_type=MESH,
        )
        for delta in range(4)
    ]
    for delta in (2, 1, 3, 0):
        mate_copies[delta].start()

    load_low.wait()
    begin(LOW)
    load_mid.wait()
    begin(MID)

    x_copies = {}
    for delta in (2, 1, 3, 0):
        load_own[delta].wait()
        mate_copies[delta].wait_recv()
        sum_buf[delta] = (
            own_buf[delta].astype(jnp.float32) + mate_buf[delta].astype(jnp.float32)
        ).astype(jnp.bfloat16)
        if delta:
            x_copies[delta] = pltpu.make_async_remote_copy(
                src_ref=sum_buf.at[delta],
                dst_ref=x_buf.at[delta - 1],
                send_sem=x_send.at[delta - 1],
                recv_sem=x_recv.at[delta - 1],
                device_id=(d, 2 * rem(x + delta, 4) + core),
                device_id_type=MESH,
            )
            x_copies[delta].start()

    load_w.wait()
    load_res.wait()

    def own_top():
        for delta in (1, 2, 3):
            x_copies[delta].wait_recv()
        total = res_buf[...].astype(jnp.float32) + sum_buf[0].astype(jnp.float32)
        for delta in (1, 2, 3):
            total = total + x_buf[delta - 1].astype(jnp.float32)
        blocks[TOP, 0, 0] = total.astype(jnp.bfloat16)

    def send_cot():
        for j in range(2):
            slot_y, slot_z = slot_of(2 * s + j)
            rows = cot.at[pl.ds(128 * j, 128)]
            pltpu.make_async_copy(rows, cot_buf.at[slot_y, slot_z], cot_recv).start()

            @pl.loop(1, 8)
            def _(step):
                pltpu.make_async_remote_copy(
                    src_ref=rows,
                    dst_ref=cot_buf.at[slot_y, slot_z],
                    send_sem=cot_send,
                    recv_sem=cot_recv,
                    device_id=(d, rem(s + step, 8)),
                    device_id_type=MESH,
                ).start()

    def product_of(kind, i, j, ni, nj):
        rows = blocks[kind, pl.ds(i, ni), j:j + nj].reshape(128 * ni * nj, 1024)
        product = jnp.dot(rows, w_buf[kind], preferred_element_type=jnp.float32)
        return product.reshape(ni, nj, 128, 512)

    def joined_part(kind, i, j, ni, nj):
        at = (pl.ds(i, ni), slice(j, j + nj))
        product = product_of(kind, i, j, ni, nj)
        joined[at] = product if kind == LOW else joined[at] + product

    def joined_near(kind):
        @pl.loop(0, 3)
        def _(i):
            joined_part(kind, i, 0, 1, 3)

    def joined_far(kind):
        joined_part(kind, 3, 0, 1, 3)
        joined_part(kind, 0, 3, 4, 1)

    def grad_all(kind):
        @pl.loop(0, 4)
        def _(piece):
            features = pl.ds(pl.multiple_of(256 * piece, 256), 256)
            grad_buf[kind, features] = lax.dot_general(
                blocks[kind, :, :, :, features].reshape(2048, 256),
                cot_buf[...].reshape(2048, 512),
                (((0,), (0,)), ((), ())),
                preferred_element_type=jnp.float32,
            )

        pltpu.make_async_copy(grad_buf.at[kind], grad.at[kind], grad_sem.at[kind]).start()

    def pair_part(i, j):
        there = div(rem(pack_of(i, j), 4), 2)

        @pl.when(there != core)
        def _():
            part_buf[i, j] = joined[i, j].astype(jnp.bfloat16)
            pltpu.make_async_remote_copy(
                src_ref=part_buf.at[i, j],
                dst_ref=mate_part.at[i, j],
                send_sem=pair_send,
                recv_sem=pair_recv.at[i, j],
                device_id=mate,
                device_id_type=MESH,
            ).start()

    def send_part(i, j):
        pack = pack_of(i, j)
        owner = div(pack, 2)
        there = owner_buf.at[rem(pack, 2), x]

        @pl.when(rem(owner, 2) == core)
        def _():
            pltpu.make_async_copy(
                mate_part.at[i, j], mate_part.at[i, j], pair_recv.at[i, j]
            ).wait()
            total = joined[i, j] + mate_part[i, j].astype(jnp.float32)
            part_buf[i, j] = total.astype(jnp.bfloat16)

        @pl.when(owner == s)
        def _():
            pltpu.make_async_copy(part_buf.at[i, j], there, part_recv.at[rem(pack, 2)]).start()

        @pl.when((owner != s) & (rem(owner, 2) == core))
        def _():
            pltpu.make_async_remote_copy(
                src_ref=part_buf.at[i, j],
                dst_ref=there,
                send_sem=part_send,
                recv_sem=part_recv.at[rem(pack, 2)],
                device_id=(d, owner),
                device_id_type=MESH,
            ).start()

    NEAR = [(i, j) for i in range(3) for j in range(3)]
    FAR_ROW = [(3, j) for j in range(3)]
    FAR_COLUMN = [(i, 3) for i in range(4)]

    def each(f, packs):
        for i, j in packs:
            f(i, j)

    own_group = []
    for j in range(2):
        slot_y, slot_z = slot_of(2 * s + j)
        own_group.append(jnp.where(slot_z == 3, 2, jnp.where(slot_y == 3, 1, 0)))

    def route(group):
        for j in range(2):

            @pl.when(own_group[j] == group)
            def _():
                pltpu.make_async_copy(owner_buf.at[j], owner_buf.at[j], part_recv.at[j]).wait()
                total = owner_buf[j, 0].astype(jnp.float32)
                for t in range(1, 4):
                    total = total + owner_buf[j, t].astype(jnp.float32)
                slots = jnp.dot(
                    select_buf[j], total.astype(jnp.bfloat16), preferred_element_type=jnp.float32
                )
                slot_buf[j] = slots.astype(jnp.bfloat16).reshape(16, 32, 512)
                there = routed.at[0, j, :, pl.ds(pl.multiple_of(d * 512, 512), 512)]
                pltpu.make_async_copy(slot_buf.at[j, d], there, route_recv).start()

                @pl.loop(1, 16)
                def _(step):
                    shard = rem(d + step, 16)
                    pltpu.make_async_remote_copy(
                        src_ref=slot_buf.at[j, shard],
                        dst_ref=there,
                        send_sem=route_send,
                        recv_sem=route_recv,
                        device_id=(shard, s),
                        device_id_type=MESH,
                    ).start()

    spread(LOW)
    spread(MID)
    own_top()
    begin(TOP)
    send_cot()
    for kind in (LOW, MID):
        relay(kind, 0)
    relay(LOW, 2)
    relay(LOW, 1)
    joined_near(LOW)
    spread(TOP)
    relay(MID, 2)
    relay(MID, 1)
    far_z(LOW)
    far_z(MID)
    far_y(LOW)
    joined_near(MID)
    far_z(TOP)
    relay(TOP, 0)
    relay(TOP, 2)
    relay(TOP, 1)
    far_y(MID)
    far_y(TOP)
    joined_near(TOP)
    each(pair_part, NEAR)
    relay(LOW, 3)
    each(send_part, NEAR)
    finish(LOW, range(4))
    joined_far(LOW)
    relay(MID, 3)
    pltpu.make_async_copy(cot_buf, cot_buf, cot_recv).wait()
    finish(MID, range(4))
    joined_far(MID)
    relay(TOP, 3)
    route(0)
    for slot in range(3):
        then_y[TOP][slot].finish()
    joined_part(TOP, 3, 0, 1, 3)
    each(pair_part, FAR_ROW)
    for slot in range(3):
        then_z[TOP][slot].finish()
    each(send_part, FAR_ROW)
    finish(TOP, (3,))
    joined_part(TOP, 0, 3, 4, 1)
    each(pair_part, FAR_COLUMN)
    grad_all(LOW)
    each(send_part, FAR_COLUMN)
    route(1)
    grad_all(MID)
    route(2)
    grad_all(TOP)

    def sent_bytes(count):
        return joined.at[:, :, pl.ds(0, 8 * count)]

    for delta in range(4):
        mate_copies[delta].wait_send()
    for delta in (1, 2, 3):
        x_copies[delta].wait_send()
    for kind in range(3):
        sent = sent_bytes(15)
        pltpu.make_async_copy(sent, sent, ring_send.at[kind]).wait()
    for count, sem in ((7, cot_send), (3, part_send), (4, pair_send)):
        sent = sent_bytes(count)
        pltpu.make_async_copy(sent, sent, sem).wait()
    for kind in range(3):
        pltpu.make_async_copy(grad_buf.at[kind], grad.at[kind], grad_sem.at[kind]).wait()
    sent = slot_buf.at[:, pl.ds(0, 15)]
    pltpu.make_async_copy(sent, sent, route_send).wait()
    pltpu.make_async_copy(slot_buf, slot_buf, route_recv).wait()


def local(
    residual, partials, low_features, mid_features, join_weight, lengths, shard_of, joined_cotangent
):
    bf16, f32 = jnp.bfloat16, jnp.float32
    hbm = pl.BlockSpec(memory_space=pl.ANY)
    dma = pltpu.SemaphoreType.DMA
    return pl.pallas_call(
        kernel,
        out_shape=(
            jax.ShapeDtypeStruct((1, 2, 32, 8192), bf16),
            jax.ShapeDtypeStruct((3, 1024, 512), f32),
        ),
        in_specs=[hbm] * 8,
        out_specs=(hbm, hbm),
        scratch_shapes=[
            pltpu.VMEM((3, 4, 4, 128, 1024), bf16),
            pltpu.VMEM((3, 1024, 512), bf16),
            pltpu.VMEM((4, 4, 128, 512), bf16),
            pltpu.VMEM((4, 128, 1024), bf16),
            pltpu.VMEM((4, 128, 1024), bf16),
            pltpu.VMEM((4, 128, 1024), bf16),
            pltpu.VMEM((3, 128, 1024), bf16),
            pltpu.VMEM((128, 1024), bf16),
            pltpu.VMEM((4, 4, 128, 512), f32),
            pltpu.VMEM((4, 4, 128, 512), bf16),
            pltpu.VMEM((2, 4, 128, 512), bf16),
            pltpu.VMEM((2, 16, 32, 512), bf16),
            pltpu.VMEM((2, 512, 128), bf16),
            pltpu.VMEM((3, 1024, 512), f32),
            pltpu.VMEM((2, 16, 5), jnp.int32),
            pltpu.VMEM((4, 4, 128, 512), bf16),
            dma((10,)),
            dma((4,)), dma((4,)),
            dma((3,)), dma((3,)),
            dma((3,)), dma((3, 10, 4)),
            dma, dma,
            dma, dma((2,)),
            dma, dma((4, 4)),
            dma, dma,
            dma((3,)),
        ],
        compiler_params=pltpu.CompilerParams(
            collective_id=0, has_side_effects=True, vmem_limit_bytes=56 * 1024 * 1024
        ),
    )(residual, partials, low_features, mid_features, join_weight, joined_cotangent, lengths, shard_of)


def solution(mesh):
    placed = (
        P("dp", "tensor"),
        P("tensor", "dp", None),
        P("dp", "tensor"),
        P("dp", "tensor"),
        P(None, "tensor", "dp"),
        P(),
        P(),
        P("tensor", "dp"),
    )
    return jax.shard_map(
        local,
        mesh=mesh,
        in_specs=placed,
        out_specs=(P("dp", "tensor", None, None), P(None, "tensor", "dp")),
        check_vma=False,
    )
```

```python
import jax
import jax.numpy as jnp
from jax import lax
from jax.experimental import pallas as pl
from jax.experimental.pallas import tpu as pltpu
from jax.sharding import PartitionSpec as P

MESH = pl.DeviceIdType.MESH

FAR_SLOT = (0, 1, 3, 2)
LOW, MID, TOP = 0, 1, 2


def lut(values, index):
    out = jnp.int32(values[0])
    for i in range(1, len(values)):
        step = values[i] - values[i - 1]
        if step:
            out = out + jnp.where(index >= i, jnp.int32(step), jnp.int32(0))
    return out


def div(a, b):
    return lax.div(a, jnp.int32(b))


def rem(a, b):
    return lax.rem(a, jnp.int32(b))


def kernel(
    residual, partials, low, mid, weight, cot, lengths, shards,
    routed, grad,
    blocks, w_buf, cot_buf, mate_buf, own_buf, sum_buf, x_buf, res_buf,
    joined, part_buf, owner_buf, slot_buf, select_buf, plan_buf, mate_part,
    load_sem, mate_send, mate_recv, x_send, x_recv, ring_send, ring_recv,
    cot_send, cot_recv, part_send, part_recv, pair_send, pair_recv, route_send, route_recv,
):
    d = lax.axis_index("dp")
    s = lax.axis_index("tensor")
    y, z = div(d, 4), rem(d, 4)
    x, core = div(s, 2), rem(s, 2)

    def slot_of(pack):
        return (
            lut(FAR_SLOT, rem(div(pack, 4) - y + 4, 4)),
            lut(FAR_SLOT, rem(rem(pack, 4) - z + 4, 4)),
        )

    def pack_of(i, j):
        return 4 * rem(y + FAR_SLOT[i], 4) + rem(z + FAR_SLOT[j], 4)

    ahead = (4 * rem(y + 1, 4) + z, 4 * y + rem(z + 1, 4))
    behind = (4 * rem(y + 3, 4) + z, 4 * y + rem(z + 3, 4))

    class Move:
        def __init__(self, kind, axis, half, fixed, op):
            self.kind, self.axis, self.half, self.fixed, self.op = kind, axis, half, fixed, op

        def at(self, slot, first, count):
            rows = pl.ds(64 * self.half + first, count)
            if self.axis == 0:
                return blocks.at[self.kind, slot, self.fixed, rows]
            return blocks.at[self.kind, self.fixed, slot, rows]

        def send(self, src, dst, sem, device):
            pltpu.make_async_remote_copy(
                src_ref=src,
                dst_ref=dst,
                send_sem=ring_send.at[self.kind],
                recv_sem=ring_recv.at[self.kind, self.op, sem],
                device_id=(device, s),
                device_id_type=MESH,
            ).start()

        def wait(self, ref, sem):
            pltpu.make_async_copy(ref, ref, ring_recv.at[self.kind, self.op, sem]).wait()

        def start(self):
            self.send(self.at(0, 0, 64), self.at(2, 0, 64), 0, ahead[self.axis])
            self.send(self.at(0, 0, 64), self.at(1, 0, 64), 1, behind[self.axis])

        def relay_ahead(self):
            self.wait(self.at(2, 0, 64), 0)
            self.send(self.at(2, 0, 32), self.at(3, 0, 32), 2, ahead[self.axis])

        def relay_behind(self):
            self.wait(self.at(1, 0, 64), 1)
            self.send(self.at(1, 32, 32), self.at(3, 32, 32), 3, behind[self.axis])

        def finish(self):
            self.wait(self.at(3, 0, 32), 2)
            self.wait(self.at(3, 32, 32), 3)

    first_y = [Move(kind, 0, 0, 0, 0) for kind in range(3)]
    first_z = [Move(kind, 1, 1, 0, 1) for kind in range(3)]
    then_z = [[Move(kind, 1, 0, i, 2 + i) for i in range(4)] for kind in range(3)]
    then_y = [[Move(kind, 0, 1, j, 6 + j) for j in range(4)] for kind in range(3)]

    def begin(kind):
        first_y[kind].start()
        first_z[kind].start()
        then_z[kind][0].start()
        then_y[kind][0].start()

    def spread(kind):
        first_y[kind].relay_ahead()
        then_z[kind][2].start()
        first_z[kind].relay_ahead()
        then_y[kind][2].start()
        first_y[kind].relay_behind()
        then_z[kind][1].start()
        first_z[kind].relay_behind()
        then_y[kind][1].start()

    def far_z(kind):
        first_y[kind].finish()
        then_z[kind][3].start()

    def far_y(kind):
        first_z[kind].finish()
        then_y[kind][3].start()

    def relay(kind, slot):
        then_z[kind][slot].relay_ahead()
        then_y[kind][slot].relay_ahead()
        then_z[kind][slot].relay_behind()
        then_y[kind][slot].relay_behind()

    def finish(kind, slots):
        for slot in slots:
            then_z[kind][slot].finish()
            then_y[kind][slot].finish()

    load_low = pltpu.make_async_copy(low, blocks.at[LOW, 0, 0], load_sem.at[0])
    load_mid = pltpu.make_async_copy(mid, blocks.at[MID, 0, 0], load_sem.at[1])
    load_lengths = pltpu.make_async_copy(lengths, plan_buf.at[0], load_sem.at[8])
    load_shards = pltpu.make_async_copy(shards, plan_buf.at[1], load_sem.at[9])
    load_res = pltpu.make_async_copy(residual, res_buf, load_sem.at[2])
    load_w = pltpu.make_async_copy(weight, w_buf, load_sem.at[3])

    def columns(delta, which):
        chip = rem(x + delta, 4)
        start = pl.multiple_of((2 * chip + which) * 1024, 1024)
        return partials.at[0, :, pl.ds(start, 1024)]

    load_own = [
        pltpu.make_async_copy(columns(delta, core), own_buf.at[delta], load_sem.at[4 + delta])
        for delta in range(4)
    ]
    load_low.start()
    load_lengths.start()
    load_shards.start()
    for delta in (2, 1, 3, 0):
        load_own[delta].start()
    load_mid.start()
    load_res.start()
    load_w.start()

    barrier = pltpu.get_barrier_semaphore()

    @pl.loop(1, 16)
    def _(step):
        pl.semaphore_signal(
            barrier, inc=1, device_id=(rem(d + step, 16), s), device_id_type=MESH
        )

    @pl.loop(1, 8)
    def _(step):
        pl.semaphore_signal(
            barrier, inc=1, device_id=(d, rem(s + step, 8)), device_id_type=MESH
        )

    load_lengths.wait()
    load_shards.wait()

    for j in range(2):
        pack = 2 * s + j
        row = lax.broadcasted_iota(jnp.int32, (512, 128), 0)
        token = lax.broadcasted_iota(jnp.int32, (512, 128), 1)
        shard = jnp.right_shift(row, 5)
        offset = jnp.bitwise_and(row, 31)
        source = jnp.full((512, 128), -1, jnp.int32)
        start = jnp.zeros((1, 1), jnp.int32)
        mine = lax.broadcasted_iota(jnp.int32, (5, 16), 1) == pack
        counts = jnp.sum(jnp.where(mine, plan_buf[0], 0), axis=1, keepdims=True)
        places = jnp.sum(jnp.where(mine, plan_buf[1], 0), axis=1, keepdims=True)
        for conv in range(5):
            count = counts[conv:conv + 1]
            here = (shard == places[conv:conv + 1]) & (offset < count)
            source = jnp.where(here, start + offset, source)
            start = start + count
        select_buf[j] = jnp.where(source == token, 1.0, 0.0).astype(jnp.bfloat16)

    pl.semaphore_wait(barrier, 22)

    mate = (d, s + 1 - 2 * core)
    mate_copies = [
        pltpu.make_async_remote_copy(
            src_ref=columns(delta, 1 - core),
            dst_ref=mate_buf.at[delta],
            send_sem=mate_send.at[delta],
            recv_sem=mate_recv.at[delta],
            device_id=mate,
            device_id_type=MESH,
        )
        for delta in range(4)
    ]
    for delta in (2, 1, 3, 0):
        mate_copies[delta].start()

    load_low.wait()
    begin(LOW)
    load_mid.wait()
    begin(MID)

    x_copies = {}
    for delta in (2, 1, 3, 0):
        load_own[delta].wait()
        mate_copies[delta].wait_recv()
        sum_buf[delta] = (
            own_buf[delta].astype(jnp.float32) + mate_buf[delta].astype(jnp.float32)
        ).astype(jnp.bfloat16)
        if delta:
            x_copies[delta] = pltpu.make_async_remote_copy(
                src_ref=sum_buf.at[delta],
                dst_ref=x_buf.at[delta - 1],
                send_sem=x_send.at[delta - 1],
                recv_sem=x_recv.at[delta - 1],
                device_id=(d, 2 * rem(x + delta, 4) + core),
                device_id_type=MESH,
            )
            x_copies[delta].start()

    load_w.wait()
    load_res.wait()

    def own_top():
        for delta in (1, 2, 3):
            x_copies[delta].wait_recv()
        total = res_buf[...].astype(jnp.float32) + sum_buf[0].astype(jnp.float32)
        for delta in (1, 2, 3):
            total = total + x_buf[delta - 1].astype(jnp.float32)
        blocks[TOP, 0, 0] = total.astype(jnp.bfloat16)

    def send_cot():
        for j in range(2):
            slot_y, slot_z = slot_of(2 * s + j)
            rows = cot.at[pl.ds(128 * j, 128)]
            pltpu.make_async_copy(rows, cot_buf.at[slot_y, slot_z], cot_recv).start()

            @pl.loop(1, 8)
            def _(step):
                pltpu.make_async_remote_copy(
                    src_ref=rows,
                    dst_ref=cot_buf.at[slot_y, slot_z],
                    send_sem=cot_send,
                    recv_sem=cot_recv,
                    device_id=(d, rem(s + step, 8)),
                    device_id_type=MESH,
                ).start()

    def product_of(kind, i, j, ni, nj):
        rows = blocks[kind, pl.ds(i, ni), j:j + nj].reshape(128 * ni * nj, 1024)
        product = jnp.dot(rows, w_buf[kind], preferred_element_type=jnp.float32)
        return product.reshape(ni, nj, 128, 512)

    def joined_part(kind, i, j, ni, nj):
        at = (pl.ds(i, ni), slice(j, j + nj))
        product = product_of(kind, i, j, ni, nj)
        joined[at] = product if kind == LOW else joined[at] + product

    def joined_near(kind):
        @pl.loop(0, 3)
        def _(i):
            joined_part(kind, i, 0, 1, 3)

    def joined_far(kind):
        joined_part(kind, 3, 0, 1, 3)
        joined_part(kind, 0, 3, 4, 1)

    def grad_all(kind):
        @pl.loop(0, 4)
        def _(piece):
            features = pl.ds(pl.multiple_of(256 * piece, 256), 256)
            grad[kind, features] = lax.dot_general(
                blocks[kind, :, :, :, features].reshape(2048, 256),
                cot_buf[...].reshape(2048, 512),
                (((0,), (0,)), ((), ())),
                preferred_element_type=jnp.float32,
            )

    def pair_part(i, j):
        there = div(rem(pack_of(i, j), 4), 2)

        @pl.when(there != core)
        def _():
            part_buf[i, j] = joined[i, j].astype(jnp.bfloat16)
            pltpu.make_async_remote_copy(
                src_ref=part_buf.at[i, j],
                dst_ref=mate_part.at[i, j],
                send_sem=pair_send,
                recv_sem=pair_recv.at[i, j],
                device_id=mate,
                device_id_type=MESH,
            ).start()

    def send_part(i, j):
        pack = pack_of(i, j)
        owner = div(pack, 2)
        there = owner_buf.at[rem(pack, 2), x]

        @pl.when(rem(owner, 2) == core)
        def _():
            pltpu.make_async_copy(
                mate_part.at[i, j], mate_part.at[i, j], pair_recv.at[i, j]
            ).wait()
            total = joined[i, j] + mate_part[i, j].astype(jnp.float32)
            part_buf[i, j] = total.astype(jnp.bfloat16)

        @pl.when(owner == s)
        def _():
            pltpu.make_async_copy(part_buf.at[i, j], there, part_recv.at[rem(pack, 2)]).start()

        @pl.when((owner != s) & (rem(owner, 2) == core))
        def _():
            pltpu.make_async_remote_copy(
                src_ref=part_buf.at[i, j],
                dst_ref=there,
                send_sem=part_send,
                recv_sem=part_recv.at[rem(pack, 2)],
                device_id=(d, owner),
                device_id_type=MESH,
            ).start()

    NEAR = [(i, j) for i in range(3) for j in range(3)]
    FAR_ROW = [(3, j) for j in range(3)]
    FAR_COLUMN = [(i, 3) for i in range(4)]

    def each(f, packs):
        for i, j in packs:
            f(i, j)

    own_group = []
    for j in range(2):
        slot_y, slot_z = slot_of(2 * s + j)
        own_group.append(jnp.where(slot_z == 3, 2, jnp.where(slot_y == 3, 1, 0)))

    def route(group):
        for j in range(2):

            @pl.when(own_group[j] == group)
            def _():
                pltpu.make_async_copy(owner_buf.at[j], owner_buf.at[j], part_recv.at[j]).wait()
                total = owner_buf[j, 0].astype(jnp.float32)
                for t in range(1, 4):
                    total = total + owner_buf[j, t].astype(jnp.float32)
                slots = jnp.dot(
                    select_buf[j], total.astype(jnp.bfloat16), preferred_element_type=jnp.float32
                )
                slot_buf[j] = slots.astype(jnp.bfloat16).reshape(16, 32, 512)
                there = routed.at[0, j, :, pl.ds(pl.multiple_of(d * 512, 512), 512)]
                pltpu.make_async_copy(slot_buf.at[j, d], there, route_recv).start()

                @pl.loop(1, 16)
                def _(step):
                    shard = rem(d + step, 16)
                    pltpu.make_async_remote_copy(
                        src_ref=slot_buf.at[j, shard],
                        dst_ref=there,
                        send_sem=route_send,
                        recv_sem=route_recv,
                        device_id=(shard, s),
                        device_id_type=MESH,
                    ).start()

    spread(LOW)
    spread(MID)
    own_top()
    begin(TOP)
    send_cot()
    for kind in (LOW, MID):
        relay(kind, 0)
    relay(LOW, 2)
    relay(LOW, 1)
    joined_near(LOW)
    spread(TOP)
    relay(MID, 2)
    relay(MID, 1)
    far_z(LOW)
    far_z(MID)
    far_y(LOW)
    joined_near(MID)
    far_z(TOP)
    relay(TOP, 0)
    relay(TOP, 2)
    relay(TOP, 1)
    far_y(MID)
    far_y(TOP)
    joined_near(TOP)
    each(pair_part, NEAR)
    relay(LOW, 3)
    each(send_part, NEAR)
    finish(LOW, range(4))
    joined_far(LOW)
    relay(MID, 3)
    pltpu.make_async_copy(cot_buf, cot_buf, cot_recv).wait()
    finish(MID, range(4))
    joined_far(MID)
    relay(TOP, 3)
    route(0)
    for slot in range(3):
        then_y[TOP][slot].finish()
    joined_part(TOP, 3, 0, 1, 3)
    each(pair_part, FAR_ROW)
    for slot in range(3):
        then_z[TOP][slot].finish()
    each(send_part, FAR_ROW)
    finish(TOP, (3,))
    joined_part(TOP, 0, 3, 4, 1)
    each(pair_part, FAR_COLUMN)
    grad_all(LOW)
    each(send_part, FAR_COLUMN)
    route(1)
    grad_all(MID)
    route(2)
    grad_all(TOP)

    def sent_bytes(count):
        return joined.at[:, :, pl.ds(0, 8 * count)]

    for delta in range(4):
        mate_copies[delta].wait_send()
    for delta in (1, 2, 3):
        x_copies[delta].wait_send()
    for kind in range(3):
        sent = sent_bytes(15)
        pltpu.make_async_copy(sent, sent, ring_send.at[kind]).wait()
    for count, sem in ((7, cot_send), (3, part_send), (4, pair_send)):
        sent = sent_bytes(count)
        pltpu.make_async_copy(sent, sent, sem).wait()
    sent = slot_buf.at[:, pl.ds(0, 15)]
    pltpu.make_async_copy(sent, sent, route_send).wait()
    pltpu.make_async_copy(slot_buf, slot_buf, route_recv).wait()


def local(
    residual, partials, low_features, mid_features, join_weight, lengths, shard_of, joined_cotangent
):
    bf16, f32 = jnp.bfloat16, jnp.float32
    hbm = pl.BlockSpec(memory_space=pl.ANY)
    vmem = pl.BlockSpec(memory_space=pltpu.VMEM)
    dma = pltpu.SemaphoreType.DMA
    return pl.pallas_call(
        kernel,
        out_shape=(
            pltpu.VMEM((1, 2, 32, 8192), bf16),
            pltpu.VMEM((3, 1024, 512), f32),
        ),
        in_specs=[hbm] * 8,
        out_specs=(vmem, vmem),
        scratch_shapes=[
            pltpu.VMEM((3, 4, 4, 128, 1024), bf16),
            pltpu.VMEM((3, 1024, 512), bf16),
            pltpu.VMEM((4, 4, 128, 512), bf16),
            pltpu.VMEM((4, 128, 1024), bf16),
            pltpu.VMEM((4, 128, 1024), bf16),
            pltpu.VMEM((4, 128, 1024), bf16),
            pltpu.VMEM((3, 128, 1024), bf16),
            pltpu.VMEM((128, 1024), bf16),
            pltpu.VMEM((4, 4, 128, 512), f32),
            pltpu.VMEM((4, 4, 128, 512), bf16),
            pltpu.VMEM((2, 4, 128, 512), bf16),
            pltpu.VMEM((2, 16, 32, 512), bf16),
            pltpu.VMEM((2, 512, 128), bf16),
            pltpu.VMEM((2, 5, 16), jnp.int32),
            pltpu.VMEM((4, 4, 128, 512), bf16),
            dma((10,)),
            dma((4,)), dma((4,)),
            dma((3,)), dma((3,)),
            dma((3,)), dma((3, 10, 4)),
            dma, dma,
            dma, dma((2,)),
            dma, dma((4, 4)),
            dma, dma,
        ],
        compiler_params=pltpu.CompilerParams(
            collective_id=0, has_side_effects=True, vmem_limit_bytes=48 * 1024 * 1024
        ),
    )(residual, partials, low_features, mid_features, join_weight, joined_cotangent, lengths.T, shard_of.T)


def solution(mesh):
    placed = (
        P("dp", "tensor"),
        P("tensor", "dp", None),
        P("dp", "tensor"),
        P("dp", "tensor"),
        P(None, "tensor", "dp"),
        P(),
        P(),
        P("tensor", "dp"),
    )
    return jax.shard_map(
        local,
        mesh=mesh,
        in_specs=placed,
        out_specs=(P("dp", "tensor", None, None), P(None, "tensor", "dp")),
        check_vma=False,
    )
```

```python
import jax
import jax.numpy as jnp
from jax import lax
from jax.experimental import pallas as pl
from jax.experimental.pallas import tpu as pltpu
from jax.sharding import PartitionSpec as P

MESH = pl.DeviceIdType.MESH

FAR_SLOT = (0, 1, 3, 2)
LOW, MID, TOP = 0, 1, 2


def lut(values, index):
    out = jnp.int32(values[0])
    for i in range(1, len(values)):
        step = values[i] - values[i - 1]
        if step:
            out = out + jnp.where(index >= i, jnp.int32(step), jnp.int32(0))
    return out


def div(a, b):
    return lax.div(a, jnp.int32(b))


def rem(a, b):
    return lax.rem(a, jnp.int32(b))


def kernel(
    residual, partials, low, mid, weight, cot, lengths, shards,
    routed, grad,
    blocks, w_buf, cot_buf, mate_buf, own_buf, sum_buf, x_buf, res_buf,
    joined, part_buf, owner_buf, slot_buf, select_buf, plan_buf, mate_part,
    load_sem, mate_send, mate_recv, x_send, x_recv, ring_send, ring_recv,
    cot_send, cot_recv, part_send, part_recv, pair_send, pair_recv, route_send, route_recv,
):
    d = lax.axis_index("dp")
    s = lax.axis_index("tensor")
    y, z = div(d, 4), rem(d, 4)
    x, core = div(s, 2), rem(s, 2)

    def slot_of(pack):
        return (
            lut(FAR_SLOT, rem(div(pack, 4) - y + 4, 4)),
            lut(FAR_SLOT, rem(rem(pack, 4) - z + 4, 4)),
        )

    def pack_of(i, j):
        return 4 * rem(y + FAR_SLOT[i], 4) + rem(z + FAR_SLOT[j], 4)

    ahead = (4 * rem(y + 1, 4) + z, 4 * y + rem(z + 1, 4))
    behind = (4 * rem(y + 3, 4) + z, 4 * y + rem(z + 3, 4))

    class Move:
        def __init__(self, kind, axis, half, fixed, op):
            self.kind, self.axis, self.half, self.fixed, self.op = kind, axis, half, fixed, op

        def at(self, slot, first, count):
            rows = pl.ds(64 * self.half + first, count)
            if self.axis == 0:
                return blocks.at[self.kind, slot, self.fixed, rows]
            return blocks.at[self.kind, self.fixed, slot, rows]

        def send(self, src, dst, sem, device):
            pltpu.make_async_remote_copy(
                src_ref=src,
                dst_ref=dst,
                send_sem=ring_send.at[self.kind],
                recv_sem=ring_recv.at[self.kind, self.op, sem],
                device_id=(device, s),
                device_id_type=MESH,
            ).start()

        def wait(self, ref, sem):
            pltpu.make_async_copy(ref, ref, ring_recv.at[self.kind, self.op, sem]).wait()

        def start(self):
            self.send(self.at(0, 0, 64), self.at(2, 0, 64), 0, ahead[self.axis])
            self.send(self.at(0, 0, 64), self.at(1, 0, 64), 1, behind[self.axis])

        def relay_ahead(self):
            self.wait(self.at(2, 0, 64), 0)
            self.send(self.at(2, 0, 32), self.at(3, 0, 32), 2, ahead[self.axis])

        def relay_behind(self):
            self.wait(self.at(1, 0, 64), 1)
            self.send(self.at(1, 32, 32), self.at(3, 32, 32), 3, behind[self.axis])

        def finish(self):
            self.wait(self.at(3, 0, 32), 2)
            self.wait(self.at(3, 32, 32), 3)

    first_y = [Move(kind, 0, 0, 0, 0) for kind in range(3)]
    first_z = [Move(kind, 1, 1, 0, 1) for kind in range(3)]
    then_z = [[Move(kind, 1, 0, i, 2 + i) for i in range(4)] for kind in range(3)]
    then_y = [[Move(kind, 0, 1, j, 6 + j) for j in range(4)] for kind in range(3)]

    def begin(kind):
        first_y[kind].start()
        first_z[kind].start()
        then_z[kind][0].start()
        then_y[kind][0].start()

    def spread(kind):
        first_y[kind].relay_ahead()
        then_z[kind][2].start()
        first_z[kind].relay_ahead()
        then_y[kind][2].start()
        first_y[kind].relay_behind()
        then_z[kind][1].start()
        first_z[kind].relay_behind()
        then_y[kind][1].start()

    def far_z(kind):
        first_y[kind].finish()
        then_z[kind][3].start()

    def far_y(kind):
        first_z[kind].finish()
        then_y[kind][3].start()

    def relay(kind, slot):
        then_z[kind][slot].relay_ahead()
        then_y[kind][slot].relay_ahead()
        then_z[kind][slot].relay_behind()
        then_y[kind][slot].relay_behind()

    def finish(kind, slots):
        for slot in slots:
            then_z[kind][slot].finish()
            then_y[kind][slot].finish()

    load_low = pltpu.make_async_copy(low, blocks.at[LOW, 0, 0], load_sem.at[0])
    load_mid = pltpu.make_async_copy(mid, blocks.at[MID, 0, 0], load_sem.at[1])
    load_lengths = pltpu.make_async_copy(lengths, plan_buf.at[0], load_sem.at[8])
    load_shards = pltpu.make_async_copy(shards, plan_buf.at[1], load_sem.at[9])
    load_res = pltpu.make_async_copy(residual, res_buf, load_sem.at[2])
    load_w = pltpu.make_async_copy(weight, w_buf, load_sem.at[3])

    def columns(delta, which):
        chip = rem(x + delta, 4)
        start = pl.multiple_of((2 * chip + which) * 1024, 1024)
        return partials.at[0, :, pl.ds(start, 1024)]

    load_own = [
        pltpu.make_async_copy(columns(delta, core), own_buf.at[delta], load_sem.at[4 + delta])
        for delta in range(4)
    ]
    load_low.start()
    load_lengths.start()
    load_shards.start()
    for delta in (2, 1, 3, 0):
        load_own[delta].start()
    load_mid.start()
    load_res.start()
    load_w.start()

    barrier = pltpu.get_barrier_semaphore()

    @pl.loop(1, 16)
    def _(step):
        pl.semaphore_signal(
            barrier, inc=1, device_id=(rem(d + step, 16), s), device_id_type=MESH
        )

    @pl.loop(1, 8)
    def _(step):
        pl.semaphore_signal(
            barrier, inc=1, device_id=(d, rem(s + step, 8)), device_id_type=MESH
        )

    load_lengths.wait()
    load_shards.wait()

    for j in range(2):
        pack = 2 * s + j
        row = lax.broadcasted_iota(jnp.int32, (512, 128), 0)
        token = lax.broadcasted_iota(jnp.int32, (512, 128), 1)
        shard = jnp.right_shift(row, 5)
        offset = jnp.bitwise_and(row, 31)
        source = jnp.full((512, 128), -1, jnp.int32)
        start = jnp.zeros((1, 1), jnp.int32)
        mine = lax.broadcasted_iota(jnp.int32, (5, 16), 1) == pack
        counts = jnp.sum(jnp.where(mine, plan_buf[0], 0), axis=1, keepdims=True)
        places = jnp.sum(jnp.where(mine, plan_buf[1], 0), axis=1, keepdims=True)
        for conv in range(5):
            count = counts[conv:conv + 1]
            here = (shard == places[conv:conv + 1]) & (offset < count)
            source = jnp.where(here, start + offset, source)
            start = start + count
        select_buf[j] = jnp.where(source == token, 1.0, 0.0).astype(jnp.bfloat16)

    pl.semaphore_wait(barrier, 22)

    mate = (d, s + 1 - 2 * core)
    mate_copies = [
        pltpu.make_async_remote_copy(
            src_ref=columns(delta, 1 - core),
            dst_ref=mate_buf.at[delta],
            send_sem=mate_send.at[delta],
            recv_sem=mate_recv.at[delta],
            device_id=mate,
            device_id_type=MESH,
        )
        for delta in range(4)
    ]
    for delta in (2, 1, 3, 0):
        mate_copies[delta].start()

    load_low.wait()
    begin(LOW)
    load_mid.wait()
    begin(MID)

    x_copies = {}
    for delta in (2, 1, 3, 0):
        load_own[delta].wait()
        mate_copies[delta].wait_recv()
        sum_buf[delta] = (
            own_buf[delta].astype(jnp.float32) + mate_buf[delta].astype(jnp.float32)
        ).astype(jnp.bfloat16)
        if delta:
            x_copies[delta] = pltpu.make_async_remote_copy(
                src_ref=sum_buf.at[delta],
                dst_ref=x_buf.at[delta - 1],
                send_sem=x_send.at[delta - 1],
                recv_sem=x_recv.at[delta - 1],
                device_id=(d, 2 * rem(x + delta, 4) + core),
                device_id_type=MESH,
            )
            x_copies[delta].start()

    load_w.wait()
    load_res.wait()

    def own_top():
        for delta in (1, 2, 3):
            x_copies[delta].wait_recv()
        total = res_buf[...].astype(jnp.float32) + sum_buf[0].astype(jnp.float32)
        for delta in (1, 2, 3):
            total = total + x_buf[delta - 1].astype(jnp.float32)
        blocks[TOP, 0, 0] = total.astype(jnp.bfloat16)

    def send_cot():
        for j in range(2):
            slot_y, slot_z = slot_of(2 * s + j)
            rows = cot.at[pl.ds(128 * j, 128)]
            pltpu.make_async_copy(rows, cot_buf.at[slot_y, slot_z], cot_recv).start()

            @pl.loop(1, 8)
            def _(step):
                pltpu.make_async_remote_copy(
                    src_ref=rows,
                    dst_ref=cot_buf.at[slot_y, slot_z],
                    send_sem=cot_send,
                    recv_sem=cot_recv,
                    device_id=(d, rem(s + step, 8)),
                    device_id_type=MESH,
                ).start()

    def product_of(kind, i, j, ni, nj):
        rows = blocks[kind, pl.ds(i, ni), j:j + nj].reshape(128 * ni * nj, 1024)
        product = jnp.dot(rows, w_buf[kind], preferred_element_type=jnp.float32)
        return product.reshape(ni, nj, 128, 512)

    def joined_part(kind, i, j, ni, nj):
        at = (pl.ds(i, ni), slice(j, j + nj))
        product = product_of(kind, i, j, ni, nj)
        joined[at] = product if kind == LOW else joined[at] + product

    def joined_near(kind):
        @pl.loop(0, 3)
        def _(i):
            joined_part(kind, i, 0, 1, 3)

    def joined_far(kind):
        joined_part(kind, 3, 0, 1, 3)
        joined_part(kind, 0, 3, 4, 1)

    def grad_part(kind, features, i, ni, j, nj):
        tokens = 128 * ni * nj
        return lax.dot_general(
            blocks[kind, i:i + ni, j:j + nj, :, features].reshape(tokens, 256),
            cot_buf[i:i + ni, j:j + nj].reshape(tokens, 512),
            (((0,), (0,)), ((), ())),
            preferred_element_type=jnp.float32,
        )

    def grad_near(kind):
        @pl.loop(0, 4)
        def _(piece):
            features = pl.ds(pl.multiple_of(256 * piece, 256), 256)
            grad[kind, features] = grad_part(kind, features, 0, 3, 0, 3)

    def grad_far(kind):
        @pl.loop(0, 4)
        def _(piece):
            features = pl.ds(pl.multiple_of(256 * piece, 256), 256)
            grad[kind, features] = (
                grad[kind, features]
                + grad_part(kind, features, 3, 1, 0, 3)
                + grad_part(kind, features, 0, 4, 3, 1)
            )

    def pair_part(i, j):
        there = div(rem(pack_of(i, j), 4), 2)

        @pl.when(there != core)
        def _():
            part_buf[i, j] = joined[i, j].astype(jnp.bfloat16)
            pltpu.make_async_remote_copy(
                src_ref=part_buf.at[i, j],
                dst_ref=mate_part.at[i, j],
                send_sem=pair_send,
                recv_sem=pair_recv.at[i, j],
                device_id=mate,
                device_id_type=MESH,
            ).start()

    def send_part(i, j):
        pack = pack_of(i, j)
        owner = div(pack, 2)
        there = owner_buf.at[rem(pack, 2), x]

        @pl.when(rem(owner, 2) == core)
        def _():
            pltpu.make_async_copy(
                mate_part.at[i, j], mate_part.at[i, j], pair_recv.at[i, j]
            ).wait()
            total = joined[i, j] + mate_part[i, j].astype(jnp.float32)
            part_buf[i, j] = total.astype(jnp.bfloat16)

        @pl.when(owner == s)
        def _():
            pltpu.make_async_copy(part_buf.at[i, j], there, part_recv.at[rem(pack, 2)]).start()

        @pl.when((owner != s) & (rem(owner, 2) == core))
        def _():
            pltpu.make_async_remote_copy(
                src_ref=part_buf.at[i, j],
                dst_ref=there,
                send_sem=part_send,
                recv_sem=part_recv.at[rem(pack, 2)],
                device_id=(d, owner),
                device_id_type=MESH,
            ).start()

    NEAR = [(i, j) for i in range(3) for j in range(3)]
    FAR_ROW = [(3, j) for j in range(3)]
    FAR_COLUMN = [(i, 3) for i in range(4)]

    def each(f, packs):
        for i, j in packs:
            f(i, j)

    own_group = []
    for j in range(2):
        slot_y, slot_z = slot_of(2 * s + j)
        own_group.append(jnp.where(slot_z == 3, 2, jnp.where(slot_y == 3, 1, 0)))

    def route(group):
        for j in range(2):

            @pl.when(own_group[j] == group)
            def _():
                pltpu.make_async_copy(owner_buf.at[j], owner_buf.at[j], part_recv.at[j]).wait()
                total = owner_buf[j, 0].astype(jnp.float32)
                for t in range(1, 4):
                    total = total + owner_buf[j, t].astype(jnp.float32)
                slots = jnp.dot(
                    select_buf[j], total.astype(jnp.bfloat16), preferred_element_type=jnp.float32
                )
                slot_buf[j] = slots.astype(jnp.bfloat16).reshape(16, 32, 512)
                there = routed.at[0, j, :, pl.ds(pl.multiple_of(d * 512, 512), 512)]
                pltpu.make_async_copy(slot_buf.at[j, d], there, route_recv).start()

                @pl.loop(1, 16)
                def _(step):
                    shard = rem(d + step, 16)
                    pltpu.make_async_remote_copy(
                        src_ref=slot_buf.at[j, shard],
                        dst_ref=there,
                        send_sem=route_send,
                        recv_sem=route_recv,
                        device_id=(shard, s),
                        device_id_type=MESH,
                    ).start()

    spread(LOW)
    spread(MID)
    own_top()
    begin(TOP)
    send_cot()
    for kind in (LOW, MID):
        relay(kind, 0)
    relay(LOW, 2)
    relay(LOW, 1)
    joined_near(LOW)
    spread(TOP)
    relay(MID, 2)
    relay(MID, 1)
    far_z(LOW)
    far_z(MID)
    far_y(LOW)
    joined_near(MID)
    relay(TOP, 0)
    far_y(MID)
    relay(TOP, 2)
    relay(TOP, 1)
    relay(LOW, 3)
    far_z(TOP)
    far_y(TOP)
    joined_near(TOP)
    each(pair_part, NEAR)
    pltpu.make_async_copy(cot_buf, cot_buf, cot_recv).wait()
    grad_near(LOW)
    relay(MID, 3)
    each(send_part, NEAR)
    finish(LOW, range(4))
    joined_far(LOW)
    relay(TOP, 3)
    finish(MID, range(4))
    joined_far(MID)
    for slot in range(3):
        then_y[TOP][slot].finish()
    joined_part(TOP, 3, 0, 1, 3)
    each(pair_part, FAR_ROW)
    for slot in range(3):
        then_z[TOP][slot].finish()
    each(send_part, FAR_ROW)
    finish(TOP, (3,))
    joined_part(TOP, 0, 3, 4, 1)
    each(pair_part, FAR_COLUMN)
    grad_near(TOP)
    each(send_part, FAR_COLUMN)
    route(0)
    route(1)
    grad_near(MID)
    grad_far(LOW)
    grad_far(MID)
    route(2)
    grad_far(TOP)

    def sent_bytes(count):
        return joined.at[:, :, pl.ds(0, 8 * count)]

    for delta in range(4):
        mate_copies[delta].wait_send()
    for delta in (1, 2, 3):
        x_copies[delta].wait_send()
    for kind in range(3):
        sent = sent_bytes(15)
        pltpu.make_async_copy(sent, sent, ring_send.at[kind]).wait()
    for count, sem in ((7, cot_send), (3, part_send), (4, pair_send)):
        sent = sent_bytes(count)
        pltpu.make_async_copy(sent, sent, sem).wait()
    sent = slot_buf.at[:, pl.ds(0, 15)]
    pltpu.make_async_copy(sent, sent, route_send).wait()
    pltpu.make_async_copy(slot_buf, slot_buf, route_recv).wait()


def local(
    residual, partials, low_features, mid_features, join_weight, lengths, shard_of, joined_cotangent
):
    bf16, f32 = jnp.bfloat16, jnp.float32
    hbm = pl.BlockSpec(memory_space=pl.ANY)
    vmem = pl.BlockSpec(memory_space=pltpu.VMEM)
    dma = pltpu.SemaphoreType.DMA
    return pl.pallas_call(
        kernel,
        out_shape=(
            pltpu.VMEM((1, 2, 32, 8192), bf16),
            pltpu.VMEM((3, 1024, 512), f32),
        ),
        in_specs=[hbm] * 8,
        out_specs=(vmem, vmem),
        scratch_shapes=[
            pltpu.VMEM((3, 4, 4, 128, 1024), bf16),
            pltpu.VMEM((3, 1024, 512), bf16),
            pltpu.VMEM((4, 4, 128, 512), bf16),
            pltpu.VMEM((4, 128, 1024), bf16),
            pltpu.VMEM((4, 128, 1024), bf16),
            pltpu.VMEM((4, 128, 1024), bf16),
            pltpu.VMEM((3, 128, 1024), bf16),
            pltpu.VMEM((128, 1024), bf16),
            pltpu.VMEM((4, 4, 128, 512), f32),
            pltpu.VMEM((4, 4, 128, 512), bf16),
            pltpu.VMEM((2, 4, 128, 512), bf16),
            pltpu.VMEM((2, 16, 32, 512), bf16),
            pltpu.VMEM((2, 512, 128), bf16),
            pltpu.VMEM((2, 5, 16), jnp.int32),
            pltpu.VMEM((4, 4, 128, 512), bf16),
            dma((10,)),
            dma((4,)), dma((4,)),
            dma((3,)), dma((3,)),
            dma((3,)), dma((3, 10, 4)),
            dma, dma,
            dma, dma((2,)),
            dma, dma((4, 4)),
            dma, dma,
        ],
        compiler_params=pltpu.CompilerParams(
            collective_id=0, has_side_effects=True, vmem_limit_bytes=48 * 1024 * 1024
        ),
    )(residual, partials, low_features, mid_features, join_weight, joined_cotangent, lengths.T, shard_of.T)


def solution(mesh):
    placed = (
        P("dp", "tensor"),
        P("tensor", "dp", None),
        P("dp", "tensor"),
        P("dp", "tensor"),
        P(None, "tensor", "dp"),
        P(),
        P(),
        P("tensor", "dp"),
    )
    return jax.shard_map(
        local,
        mesh=mesh,
        in_specs=placed,
        out_specs=(P("dp", "tensor", None, None), P(None, "tensor", "dp")),
        check_vma=False,
    )
```

```python
import jax
import jax.numpy as jnp
from jax import lax
from jax.experimental import pallas as pl
from jax.experimental.pallas import tpu as pltpu
from jax.sharding import PartitionSpec as P

MESH = pl.DeviceIdType.MESH

FAR_SLOT = (0, 1, 3, 2)
LOW, MID, TOP = 0, 1, 2


def lut(values, index):
    out = jnp.int32(values[0])
    for i in range(1, len(values)):
        step = values[i] - values[i - 1]
        if step:
            out = out + jnp.where(index >= i, jnp.int32(step), jnp.int32(0))
    return out


def div(a, b):
    return lax.div(a, jnp.int32(b))


def rem(a, b):
    return lax.rem(a, jnp.int32(b))


def kernel(
    residual, partials, low, mid, weight, cot, lengths, shards,
    routed, grad,
    blocks, w_buf, cot_buf, mate_buf, own_buf, sum_buf, x_buf, res_buf,
    joined, part_buf, owner_buf, slot_buf, select_buf, plan_buf, mate_part,
    load_sem, mate_send, mate_recv, x_send, x_recv, ring_send, ring_recv,
    cot_send, cot_recv, part_send, part_recv, pair_send, pair_recv, route_send, route_recv,
):
    d = lax.axis_index("dp")
    s = lax.axis_index("tensor")
    y, z = div(d, 4), rem(d, 4)
    x, core = div(s, 2), rem(s, 2)

    def slot_of(pack):
        return (
            lut(FAR_SLOT, rem(div(pack, 4) - y + 4, 4)),
            lut(FAR_SLOT, rem(rem(pack, 4) - z + 4, 4)),
        )

    def pack_of(i, j):
        return 4 * rem(y + FAR_SLOT[i], 4) + rem(z + FAR_SLOT[j], 4)

    ahead = (4 * rem(y + 1, 4) + z, 4 * y + rem(z + 1, 4))
    behind = (4 * rem(y + 3, 4) + z, 4 * y + rem(z + 3, 4))

    class Move:
        def __init__(self, kind, axis, half, fixed, op):
            self.kind, self.axis, self.half, self.fixed, self.op = kind, axis, half, fixed, op

        def at(self, slot, first, count):
            rows = pl.ds(64 * self.half + first, count)
            if self.axis == 0:
                return blocks.at[self.kind, slot, self.fixed, rows]
            return blocks.at[self.kind, self.fixed, slot, rows]

        def send(self, src, dst, sem, device):
            pltpu.make_async_remote_copy(
                src_ref=src,
                dst_ref=dst,
                send_sem=ring_send.at[self.kind],
                recv_sem=ring_recv.at[self.kind, self.op, sem],
                device_id=(device, s),
                device_id_type=MESH,
            ).start()

        def wait(self, ref, sem):
            pltpu.make_async_copy(ref, ref, ring_recv.at[self.kind, self.op, sem]).wait()

        def start(self):
            self.send(self.at(0, 0, 64), self.at(2, 0, 64), 0, ahead[self.axis])
            self.send(self.at(0, 0, 64), self.at(1, 0, 64), 1, behind[self.axis])

        def relay_ahead(self):
            self.wait(self.at(2, 0, 64), 0)
            self.send(self.at(2, 0, 32), self.at(3, 0, 32), 2, ahead[self.axis])

        def relay_behind(self):
            self.wait(self.at(1, 0, 64), 1)
            self.send(self.at(1, 32, 32), self.at(3, 32, 32), 3, behind[self.axis])

        def finish(self):
            self.wait(self.at(3, 0, 32), 2)
            self.wait(self.at(3, 32, 32), 3)

    first_y = [Move(kind, 0, 0, 0, 0) for kind in range(3)]
    first_z = [Move(kind, 1, 1, 0, 1) for kind in range(3)]
    then_z = [[Move(kind, 1, 0, i, 2 + i) for i in range(4)] for kind in range(3)]
    then_y = [[Move(kind, 0, 1, j, 6 + j) for j in range(4)] for kind in range(3)]

    def begin(kind):
        first_y[kind].start()
        first_z[kind].start()
        then_z[kind][0].start()
        then_y[kind][0].start()

    def spread(kind):
        first_y[kind].relay_ahead()
        then_z[kind][2].start()
        first_z[kind].relay_ahead()
        then_y[kind][2].start()
        first_y[kind].relay_behind()
        then_z[kind][1].start()
        first_z[kind].relay_behind()
        then_y[kind][1].start()

    def far_z(kind):
        first_y[kind].finish()
        then_z[kind][3].start()

    def far_y(kind):
        first_z[kind].finish()
        then_y[kind][3].start()

    def relay_far(move):
        move[3].relay_ahead()
        move[3].relay_behind()

    def relay(kind, slot):
        then_z[kind][slot].relay_ahead()
        then_y[kind][slot].relay_ahead()
        then_z[kind][slot].relay_behind()
        then_y[kind][slot].relay_behind()

    def finish(moves):
        for move in moves:
            move.finish()

    load_low = pltpu.make_async_copy(low, blocks.at[LOW, 0, 0], load_sem.at[0])
    load_mid = pltpu.make_async_copy(mid, blocks.at[MID, 0, 0], load_sem.at[1])
    load_lengths = pltpu.make_async_copy(lengths, plan_buf.at[0], load_sem.at[8])
    load_shards = pltpu.make_async_copy(shards, plan_buf.at[1], load_sem.at[9])
    load_res = pltpu.make_async_copy(residual, res_buf, load_sem.at[2])
    load_w = pltpu.make_async_copy(weight, w_buf, load_sem.at[3])

    def columns(delta, which):
        chip = rem(x + delta, 4)
        start = pl.multiple_of((2 * chip + which) * 1024, 1024)
        return partials.at[0, :, pl.ds(start, 1024)]

    load_own = [
        pltpu.make_async_copy(columns(delta, core), own_buf.at[delta], load_sem.at[4 + delta])
        for delta in range(4)
    ]
    load_low.start()
    load_lengths.start()
    load_shards.start()
    for delta in (2, 1, 3, 0):
        load_own[delta].start()
    load_mid.start()
    load_res.start()
    load_w.start()

    barrier = pltpu.get_barrier_semaphore()

    @pl.loop(1, 16)
    def _(step):
        pl.semaphore_signal(
            barrier, inc=1, device_id=(rem(d + step, 16), s), device_id_type=MESH
        )

    @pl.loop(1, 8)
    def _(step):
        pl.semaphore_signal(
            barrier, inc=1, device_id=(d, rem(s + step, 8)), device_id_type=MESH
        )

    load_lengths.wait()
    load_shards.wait()

    for j in range(2):
        pack = 2 * s + j
        row = lax.broadcasted_iota(jnp.int32, (512, 128), 0)
        token = lax.broadcasted_iota(jnp.int32, (512, 128), 1)
        shard = jnp.right_shift(row, 5)
        offset = jnp.bitwise_and(row, 31)
        source = jnp.full((512, 128), -1, jnp.int32)
        start = jnp.zeros((1, 1), jnp.int32)
        mine = lax.broadcasted_iota(jnp.int32, (5, 16), 1) == pack
        counts = jnp.sum(jnp.where(mine, plan_buf[0], 0), axis=1, keepdims=True)
        places = jnp.sum(jnp.where(mine, plan_buf[1], 0), axis=1, keepdims=True)
        for conv in range(5):
            count = counts[conv:conv + 1]
            here = (shard == places[conv:conv + 1]) & (offset < count)
            source = jnp.where(here, start + offset, source)
            start = start + count
        select_buf[j] = jnp.where(source == token, 1.0, 0.0).astype(jnp.bfloat16)

    pl.semaphore_wait(barrier, 22)

    mate = (d, s + 1 - 2 * core)
    mate_copies = [
        pltpu.make_async_remote_copy(
            src_ref=columns(delta, 1 - core),
            dst_ref=mate_buf.at[delta],
            send_sem=mate_send.at[delta],
            recv_sem=mate_recv.at[delta],
            device_id=mate,
            device_id_type=MESH,
        )
        for delta in range(4)
    ]
    for delta in (2, 1, 3, 0):
        mate_copies[delta].start()

    load_low.wait()
    begin(LOW)
    load_mid.wait()
    begin(MID)

    x_copies = {}
    for delta in (2, 1, 3, 0):
        load_own[delta].wait()
        mate_copies[delta].wait_recv()
        sum_buf[delta] = (
            own_buf[delta].astype(jnp.float32) + mate_buf[delta].astype(jnp.float32)
        ).astype(jnp.bfloat16)
        if delta:
            x_copies[delta] = pltpu.make_async_remote_copy(
                src_ref=sum_buf.at[delta],
                dst_ref=x_buf.at[delta - 1],
                send_sem=x_send.at[delta - 1],
                recv_sem=x_recv.at[delta - 1],
                device_id=(d, 2 * rem(x + delta, 4) + core),
                device_id_type=MESH,
            )
            x_copies[delta].start()

    load_w.wait()
    load_res.wait()

    def own_top():
        for delta in (1, 2, 3):
            x_copies[delta].wait_recv()
        total = res_buf[...].astype(jnp.float32) + sum_buf[0].astype(jnp.float32)
        for delta in (1, 2, 3):
            total = total + x_buf[delta - 1].astype(jnp.float32)
        blocks[TOP, 0, 0] = total.astype(jnp.bfloat16)

    def send_cot():
        for j in range(2):
            slot_y, slot_z = slot_of(2 * s + j)
            rows = cot.at[pl.ds(128 * j, 128)]
            pltpu.make_async_copy(rows, cot_buf.at[slot_y, slot_z], cot_recv).start()

            @pl.loop(1, 8)
            def _(step):
                pltpu.make_async_remote_copy(
                    src_ref=rows,
                    dst_ref=cot_buf.at[slot_y, slot_z],
                    send_sem=cot_send,
                    recv_sem=cot_recv,
                    device_id=(d, rem(s + step, 8)),
                    device_id_type=MESH,
                ).start()

    def product_of(kind, i, j, ni, nj):
        rows = blocks[kind, pl.ds(i, ni), j:j + nj].reshape(128 * ni * nj, 1024)
        product = jnp.dot(rows, w_buf[kind], preferred_element_type=jnp.float32)
        return product.reshape(ni, nj, 128, 512)

    def joined_part(kind, i, j, ni, nj):
        at = (pl.ds(i, ni), slice(j, j + nj))
        product = product_of(kind, i, j, ni, nj)
        joined[at] = product if kind == LOW else joined[at] + product

    def joined_near(kind):
        @pl.loop(0, 3)
        def _(i):
            joined_part(kind, i, 0, 1, 3)

    def grad_part(kind, features, i, ni, j, nj):
        tokens = 128 * ni * nj
        return lax.dot_general(
            blocks[kind, i:i + ni, j:j + nj, :, features].reshape(tokens, 256),
            cot_buf[i:i + ni, j:j + nj].reshape(tokens, 512),
            (((0,), (0,)), ((), ())),
            preferred_element_type=jnp.float32,
        )

    def grad_near(kind):
        @pl.loop(0, 4)
        def _(piece):
            features = pl.ds(pl.multiple_of(256 * piece, 256), 256)
            grad[kind, features] = grad_part(kind, features, 0, 3, 0, 3)

    def grad_far(kind):
        @pl.loop(0, 4)
        def _(piece):
            features = pl.ds(pl.multiple_of(256 * piece, 256), 256)
            grad[kind, features] = (
                grad[kind, features]
                + grad_part(kind, features, 3, 1, 0, 3)
                + grad_part(kind, features, 0, 4, 3, 1)
            )

    def pair_part(i, j):
        there = div(rem(pack_of(i, j), 4), 2)

        @pl.when(there != core)
        def _():
            part_buf[i, j] = joined[i, j].astype(jnp.bfloat16)
            pltpu.make_async_remote_copy(
                src_ref=part_buf.at[i, j],
                dst_ref=mate_part.at[i, j],
                send_sem=pair_send,
                recv_sem=pair_recv.at[i, j],
                device_id=mate,
                device_id_type=MESH,
            ).start()

    def send_part(i, j):
        pack = pack_of(i, j)
        owner = div(pack, 2)
        there = owner_buf.at[rem(pack, 2), x]

        @pl.when(rem(owner, 2) == core)
        def _():
            pltpu.make_async_copy(
                mate_part.at[i, j], mate_part.at[i, j], pair_recv.at[i, j]
            ).wait()
            total = joined[i, j] + mate_part[i, j].astype(jnp.float32)
            part_buf[i, j] = total.astype(jnp.bfloat16)

        @pl.when(owner == s)
        def _():
            pltpu.make_async_copy(part_buf.at[i, j], there, part_recv.at[rem(pack, 2)]).start()

        @pl.when((owner != s) & (rem(owner, 2) == core))
        def _():
            pltpu.make_async_remote_copy(
                src_ref=part_buf.at[i, j],
                dst_ref=there,
                send_sem=part_send,
                recv_sem=part_recv.at[rem(pack, 2)],
                device_id=(d, owner),
                device_id_type=MESH,
            ).start()

    NEAR = [(i, j) for i in range(4) for j in range(3)]
    FAR_COLUMN = [(i, 3) for i in range(4)]

    def each(f, packs):
        for i, j in packs:
            f(i, j)

    own_group = []
    for j in range(2):
        slot_y, slot_z = slot_of(2 * s + j)
        own_group.append(jnp.where(slot_z == 3, 1, 0))

    def route(group):
        for j in range(2):

            @pl.when(own_group[j] == group)
            def _():
                pltpu.make_async_copy(owner_buf.at[j], owner_buf.at[j], part_recv.at[j]).wait()
                total = owner_buf[j, 0].astype(jnp.float32)
                for t in range(1, 4):
                    total = total + owner_buf[j, t].astype(jnp.float32)
                slots = jnp.dot(
                    select_buf[j], total.astype(jnp.bfloat16), preferred_element_type=jnp.float32
                )
                slot_buf[j] = slots.astype(jnp.bfloat16).reshape(16, 32, 512)
                there = routed.at[0, j, :, pl.ds(pl.multiple_of(d * 512, 512), 512)]
                pltpu.make_async_copy(slot_buf.at[j, d], there, route_recv).start()

                @pl.loop(1, 16)
                def _(step):
                    shard = rem(d + step, 16)
                    pltpu.make_async_remote_copy(
                        src_ref=slot_buf.at[j, shard],
                        dst_ref=there,
                        send_sem=route_send,
                        recv_sem=route_recv,
                        device_id=(shard, s),
                        device_id_type=MESH,
                    ).start()

    spread(LOW)
    spread(MID)
    own_top()
    begin(TOP)
    send_cot()
    for kind in (LOW, MID):
        relay(kind, 0)
    relay(LOW, 2)
    relay(LOW, 1)
    joined_near(LOW)
    spread(TOP)
    relay(MID, 2)
    relay(MID, 1)
    far_z(LOW)
    far_z(MID)
    far_y(LOW)
    joined_near(MID)
    relay(TOP, 0)
    far_y(MID)
    far_z(TOP)
    relay(TOP, 2)
    relay(TOP, 1)
    far_y(TOP)
    joined_near(TOP)
    relay_far(then_z[LOW])
    relay_far(then_z[MID])
    finish(then_y[LOW][:3])
    joined_part(LOW, 3, 0, 1, 3)
    relay_far(then_z[TOP])
    finish(then_y[MID][:3])
    joined_part(MID, 3, 0, 1, 3)
    finish(then_y[TOP][:3])
    joined_part(TOP, 3, 0, 1, 3)
    each(pair_part, NEAR)
    relay_far(then_y[LOW])
    relay_far(then_y[MID])
    each(send_part, NEAR)
    relay_far(then_y[TOP])
    pltpu.make_async_copy(cot_buf, cot_buf, cot_recv).wait()
    grad_near(LOW)
    for kind in (LOW, MID):
        finish(then_z[kind] + then_y[kind][3:])
        joined_part(kind, 0, 3, 4, 1)
    finish(then_z[TOP] + then_y[TOP][3:])
    joined_part(TOP, 0, 3, 4, 1)
    each(pair_part, FAR_COLUMN)
    each(send_part, FAR_COLUMN)
    route(0)
    grad_near(TOP)
    grad_near(MID)
    route(1)
    grad_far(LOW)
    grad_far(MID)
    grad_far(TOP)

    def sent_bytes(count):
        return joined.at[:, :, pl.ds(0, 8 * count)]

    for delta in range(4):
        mate_copies[delta].wait_send()
    for delta in (1, 2, 3):
        x_copies[delta].wait_send()
    for kind in range(3):
        sent = sent_bytes(15)
        pltpu.make_async_copy(sent, sent, ring_send.at[kind]).wait()
    for count, sem in ((7, cot_send), (3, part_send), (4, pair_send)):
        sent = sent_bytes(count)
        pltpu.make_async_copy(sent, sent, sem).wait()
    sent = slot_buf.at[:, pl.ds(0, 15)]
    pltpu.make_async_copy(sent, sent, route_send).wait()
    pltpu.make_async_copy(slot_buf, slot_buf, route_recv).wait()


def local(
    residual, partials, low_features, mid_features, join_weight, lengths, shard_of, joined_cotangent
):
    bf16, f32 = jnp.bfloat16, jnp.float32
    hbm = pl.BlockSpec(memory_space=pl.ANY)
    vmem = pl.BlockSpec(memory_space=pltpu.VMEM)
    dma = pltpu.SemaphoreType.DMA
    return pl.pallas_call(
        kernel,
        out_shape=(
            pltpu.VMEM((1, 2, 32, 8192), bf16),
            pltpu.VMEM((3, 1024, 512), f32),
        ),
        in_specs=[hbm] * 8,
        out_specs=(vmem, vmem),
        scratch_shapes=[
            pltpu.VMEM((3, 4, 4, 128, 1024), bf16),
            pltpu.VMEM((3, 1024, 512), bf16),
            pltpu.VMEM((4, 4, 128, 512), bf16),
            pltpu.VMEM((4, 128, 1024), bf16),
            pltpu.VMEM((4, 128, 1024), bf16),
            pltpu.VMEM((4, 128, 1024), bf16),
            pltpu.VMEM((3, 128, 1024), bf16),
            pltpu.VMEM((128, 1024), bf16),
            pltpu.VMEM((4, 4, 128, 512), f32),
            pltpu.VMEM((4, 4, 128, 512), bf16),
            pltpu.VMEM((2, 4, 128, 512), bf16),
            pltpu.VMEM((2, 16, 32, 512), bf16),
            pltpu.VMEM((2, 512, 128), bf16),
            pltpu.VMEM((2, 5, 16), jnp.int32),
            pltpu.VMEM((4, 4, 128, 512), bf16),
            dma((10,)),
            dma((4,)), dma((4,)),
            dma((3,)), dma((3,)),
            dma((3,)), dma((3, 10, 4)),
            dma, dma,
            dma, dma((2,)),
            dma, dma((4, 4)),
            dma, dma,
        ],
        compiler_params=pltpu.CompilerParams(
            collective_id=0, has_side_effects=True, vmem_limit_bytes=48 * 1024 * 1024
        ),
    )(residual, partials, low_features, mid_features, join_weight, joined_cotangent, lengths.T, shard_of.T)


def solution(mesh):
    placed = (
        P("dp", "tensor"),
        P("tensor", "dp", None),
        P("dp", "tensor"),
        P("dp", "tensor"),
        P(None, "tensor", "dp"),
        P(),
        P(),
        P("tensor", "dp"),
    )
    return jax.shard_map(
        local,
        mesh=mesh,
        in_specs=placed,
        out_specs=(P("dp", "tensor", None, None), P(None, "tensor", "dp")),
        check_vma=False,
    )
```
